1024 devices in a mesh: bulk: 64 (over y, x), pair: 16 (over z, core).
Axes of the slice: x: 8, y: 8, z: 8, core: 2. Of those that a mesh axis runs over, the one named last changes fastest.
Arguments:
- amps: bfloat16 [4096, 131072], P(None, ('bulk', 'pair')), may hold values from -6 to 6
- intermediate: bfloat16 [131072, 2048], P('bulk'), may hold values from -0.09375 to 0.09375
- row_irrep: int32 [4096], replicated, may hold values from 0 to 7, as said below
- kc_irrep: int32 [131072], P(('bulk', 'pair')), may hold values from 0 to 7, as said below
- row_occ: int32 [4096], P(('pair', 'bulk')), may hold values from 0 to 249
- row_vir: int32 [4096], P(('pair', 'bulk')), may hold values from 0 to 1499
- col_occ: int32 [2048], replicated, may hold values from 0 to 249
- col_vir: int32 [2048], replicated, may hold values from 0 to 1499
- occ_energy: float32 [250], replicated, may hold values from -1.5 to -0.5
- virt_energy: float32 [1500], replicated, may hold values from 0.5 to 2.5
Outputs:
- panel_update: bfloat16 [4096, 2048], P(('pair', 'bulk'))
The draws below stay inside these ranges and needn't reach their ends.
Inputs may be any that keep to these rules, and one draw needn't show every extreme that they name: `row_irrep`: constant over aligned blocks of 64 rows; every label 0 to 7 occurs. `kc_irrep`: constant over aligned blocks of 64 pairs; every label 0 to 7 occurs.
All inputs are finite; a program needn't handle non-finite values.
Results may differ from the reference program's by a relative error of at most 0.0013.
Values may be sent and summed in bfloat16 or wider, within the bound.
A program may use at most 32 MiB of HBM per device.

```python
import jax
import jax.numpy as jnp
from jax import lax

NCOL = 2048
NOCC = 250
NVIR = 1500
IRB = 64
KC_DEV = 2048
P_SIZE = 4096
K = 131072
N_BULK = 64


def block_labels(key, amount):
    labels = jax.random.randint(key, (amount // IRB,), 0, 8, dtype=jnp.int32)
    leading = jax.random.permutation(jax.random.fold_in(key, 7), 8).astype(jnp.int32)
    labels = labels.at[:8].set(leading)
    return jnp.repeat(labels, IRB, total_repeat_length=amount)


def draw_row_irrep(key, part):
    key = jax.random.fold_in(key, 1)
    return block_labels(key, P_SIZE)


def draw_kc_irrep(key, part):
    key = jax.random.fold_in(key, 2)
    return block_labels(key, K)


def touch_ends(result, own_key, smallest, top_value):
    extent = result.shape
    index_at = [jax.random.randint(jax.random.fold_in(own_key, axis), (), 0, extent[axis]) for axis in range(len(extent))]
    result = result.at[tuple(index_at)].set(smallest)
    longest = extent.index(max(extent))
    index_at[longest] = (index_at[longest] + 1) % extent[longest]
    return result.at[tuple(index_at)].set(top_value)


def block_levels(key, dims, split, low, high):
    loudness, own = 1.0, jax.random.fold_in(key, 6)
    for dim, blocks in split:
        steps = jnp.exp(jax.random.uniform(jax.random.fold_in(own, dim), (blocks,), jnp.float32, low / len(split), high / len(split)))
        loudness = loudness * jnp.repeat(steps, dims[dim] // blocks).reshape([-1 if axis == dim else 1 for axis in range(len(dims))])
    return loudness


def scatter_about(stream_key, dims, width, limit, shards=(), held_as=jnp.bfloat16):
    level = block_levels(stream_key, dims, shards, -0.22, 0.18) if shards else 1.0
    drawn = jax.random.normal(stream_key, dims, jnp.float32) * width * level
    return jnp.minimum(jnp.maximum(drawn, -limit), limit).astype(held_as)


def setup_inputs(seed: int = 0) -> dict:
    key_of = jax.random.split(jax.random.key(seed), 11)
    amps = scatter_about(key_of[0], (P_SIZE, K), 1.0, 6.0, ((1, 1024),))
    intermediate = scatter_about(key_of[1], (K, NCOL), (K // 32) ** -0.5, 0.09375, ((0, 64),))
    row_irrep = draw_row_irrep(jax.random.fold_in(key_of[10], 71), 0)
    kc_irrep = draw_kc_irrep(jax.random.fold_in(key_of[10], 71), 0)
    row_occ = touch_ends(jax.random.randint(key_of[4], (P_SIZE,), 0, NOCC), jax.random.fold_in(key_of[4], 1), 0, NOCC - 1).astype(jnp.int32)
    row_vir = touch_ends(jax.random.randint(key_of[5], (P_SIZE,), 0, NVIR), jax.random.fold_in(key_of[5], 1), 0, NVIR - 1).astype(jnp.int32)
    col_occ = touch_ends(jax.random.randint(key_of[6], (NCOL,), 0, NOCC), jax.random.fold_in(key_of[6], 1), 0, NOCC - 1).astype(jnp.int32)
    col_vir = touch_ends(jax.random.randint(key_of[7], (NCOL,), 0, NVIR), jax.random.fold_in(key_of[7], 1), 0, NVIR - 1).astype(jnp.int32)
    occ_energy = jnp.clip(jax.random.uniform(key_of[8], (NOCC,), jnp.float32, -1.5, -0.5), -1.5, -0.5)
    virt_energy = jnp.clip(jax.random.uniform(key_of[9], (NVIR,), jnp.float32, 0.5, 2.5), 0.5, 2.5)
    return dict(amps=amps, intermediate=intermediate, row_irrep=row_irrep, kc_irrep=kc_irrep, row_occ=row_occ, row_vir=row_vir, col_occ=col_occ, col_vir=col_vir, occ_energy=occ_energy, virt_energy=virt_energy)


def reference(amps, intermediate, row_irrep, kc_irrep, row_occ, row_vir, col_occ, col_vir, occ_energy, virt_energy):
    def add_block(total, index):
        begin = (index * KC_DEV).astype(jnp.int32)
        piece = lax.dynamic_slice_in_dim(amps, begin, KC_DEV, 1)
        labels = lax.dynamic_slice_in_dim(kc_irrep, begin, KC_DEV, 0)
        weights = lax.dynamic_slice_in_dim(intermediate, begin, KC_DEV, 0)
        masked = jnp.where(row_irrep[:, None] == labels[None, :], piece, jnp.zeros_like(piece))
        return total + jnp.dot(masked, weights, preferred_element_type=jnp.float32), None

    cycle_sums, _ = lax.scan(add_block, jnp.zeros((P_SIZE, NCOL), jnp.float32), jnp.arange(N_BULK, dtype=jnp.int32))
    row_gap = jnp.take(virt_energy, row_vir) - jnp.take(occ_energy, row_occ)
    col_gap = jnp.take(virt_energy, col_vir) - jnp.take(occ_energy, col_occ)
    denominator = row_gap[:, None] + col_gap[None, :]
    return (cycle_sums / denominator).astype(jnp.bfloat16)
```

```python
import functools

import jax
import jax.numpy as jnp
from jax import lax
from jax.experimental import pallas as pl
from jax.experimental.pallas import tpu as pltpu
from jax.sharding import PartitionSpec as P

MESH = pl.DeviceIdType.MESH
F32 = jnp.float32
BF16 = jnp.bfloat16

SIDE = 8
PAIRS = 16
ROWS = 4
PLANE = SIDE * SIDE
LANES = 128
IRB = 64


def split_gather(table, labels):
    size = table.shape[1]
    whole = jnp.broadcast_to(table, (16, size))
    high = whole.astype(BF16).astype(F32)
    rest = whole - high
    middle = rest.astype(BF16).astype(F32)
    low = rest - middle
    part = lax.broadcasted_iota(jnp.int32, (16, size), 0)
    parts = jnp.where(part == 0, high, jnp.where(part == 1, middle, jnp.where(part == 2, low, 0.0))).astype(BF16)
    place = lax.broadcasted_iota(jnp.int32, (size, labels.shape[1]), 0)
    chosen = jnp.where(place == labels, 1.0, 0.0).astype(BF16)
    got = jnp.dot(parts, chosen, preferred_element_type=F32)
    return got[0:1, :] + (got[1:2, :] + got[2:3, :])


def kernel(
    amps_hbm,
    weights_hbm,
    row_irrep,
    kc_irrep,
    row_occ,
    row_vir,
    col_occ,
    col_vir,
    occ_scalar,
    virt_scalar,
    occ_vector,
    virt_vector,
    out_ref,
    amps,
    weights,
    outgoing,
    regrouped,
    sums,
    first_in,
    first_out,
    second_in,
    panel,
    virt_table,
    occ_table,
    col_gap,
    amps_sem,
    weights_sem,
    pair_send,
    pair_recv,
    first_send,
    first_recv,
    second_send,
    second_recv,
):
    bulk = lax.axis_index("bulk")
    pair = lax.axis_index("pair")
    at_y, at_x = lax.div(bulk, SIDE), lax.rem(bulk, SIDE)
    columns = weights.shape[1]

    amps_copy = pltpu.make_async_copy(amps_hbm, amps, amps_sem)
    amps_copy.start()
    weights_copy = pltpu.make_async_copy(weights_hbm, weights, weights_sem)
    weights_copy.start()

    def pair_peer(step):
        return lax.rem(pair + step, PAIRS)

    def x_peer(step):
        return at_y * SIDE + lax.rem(at_x + step, SIDE)

    def y_peer(step):
        return lax.rem(at_y + step, SIDE) * SIDE + at_x

    barrier = pltpu.get_barrier_semaphore()

    @pl.loop(1, PAIRS)
    def _(step):
        pl.semaphore_signal(barrier, inc=1, device_id=(bulk, pair_peer(step)), device_id_type=MESH)

    @pl.loop(1, SIDE)
    def _(step):
        pl.semaphore_signal(barrier, inc=1, device_id=(x_peer(step), pair), device_id_type=MESH)
        pl.semaphore_signal(barrier, inc=1, device_id=(y_peer(step), pair), device_id_type=MESH)

    block = ROWS * PLANE
    new_place = lax.broadcasted_iota(jnp.int32, (block, block), 0)
    old_place = lax.broadcasted_iota(jnp.int32, (block, block), 1)
    chunk_of = new_place >> 6
    outer, inner = (new_place >> 3) & 7, new_place & 7
    even = (chunk_of & 1) == 0
    y_of, x_of = jnp.where(even, inner, outer), jnp.where(even, outer, inner)
    reorder = jnp.where(old_place == y_of * (SIDE * ROWS) + x_of * ROWS + chunk_of, 1.0, 0.0).astype(BF16)
    kc = kc_irrep[...]

    amps_copy.wait()
    pl.semaphore_wait(barrier, PAIRS - 1 + 2 * (SIDE - 1))

    def pair_copy(chunk, step):
        peer = pair_peer(step)
        return pltpu.make_async_remote_copy(
            src_ref=outgoing.at[chunk, peer],
            dst_ref=regrouped.at[chunk, :, pl.ds(pl.multiple_of(pair * LANES, LANES), LANES)],
            send_sem=pair_send.at[chunk, step],
            recv_sem=pair_recv.at[chunk, pair],
            device_id=(bulk, peer),
            device_id_type=MESH,
        )

    def pair_arrival(chunk, step):
        source = pair_peer(step)
        return pltpu.make_async_remote_copy(
            src_ref=outgoing.at[chunk, source],
            dst_ref=regrouped.at[chunk, :, pl.ds(pl.multiple_of(source * LANES, LANES), LANES)],
            send_sem=pair_send.at[chunk, step],
            recv_sem=pair_recv.at[chunk, source],
            device_id=(bulk, source),
            device_id_type=MESH,
        )

    def prepare(owner):
        kept = []
        for part in range(block // IRB):
            label = row_irrep[owner * block + part * IRB]
            keep = jnp.where(kc == label, 1.0, 0.0)
            begin = pl.multiple_of(owner * block + part * IRB, IRB)
            kept.append((amps[pl.ds(begin, IRB), :].astype(F32) * keep).astype(BF16))
        moved = jnp.dot(reorder, jnp.concatenate(kept, axis=0), preferred_element_type=F32).astype(BF16)
        for chunk in range(ROWS):
            outgoing[chunk, owner] = moved[chunk * PLANE : (chunk + 1) * PLANE, :]

    @pl.loop(1, PAIRS)
    def _(step):
        prepare(pair_peer(step))
        pair_copy(0, step).start()

    for chunk in range(1, ROWS):

        @pl.loop(1, PAIRS)
        def _(step):
            pair_copy(chunk, step).start()

    prepare(pair)
    for chunk in range(ROWS):
        regrouped[chunk, :, pl.ds(pl.multiple_of(pair * LANES, LANES), LANES)] = outgoing[chunk, pair]

    virt_table[...] = jnp.zeros_like(virt_table)
    occ_table[...] = jnp.zeros_like(occ_table)
    virt_table[:, 0 : virt_vector.shape[1]] = virt_vector[...]
    occ_table[:, 0 : occ_vector.shape[1]] = occ_vector[...]
    width = 256

    @pl.loop(0, columns // width)
    def _(tile):
        where = pl.ds(pl.multiple_of(tile * width, width), width)
        col_gap[:, where] = split_gather(virt_table[...], col_vir[:, where]) - split_gather(occ_table[...], col_occ[:, where])

    weights_copy.wait()

    def first_copy(chunk, step, arrival=False):
        mine = at_x if chunk % 2 == 0 else at_y
        to = lax.rem(mine + step, SIDE)
        source = to if arrival else mine
        return pltpu.make_async_remote_copy(
            src_ref=sums.at[chunk, pl.ds(pl.multiple_of(to * SIDE, SIDE), SIDE), :],
            dst_ref=first_in.at[chunk, source],
            send_sem=first_send.at[chunk, step],
            recv_sem=first_recv.at[chunk, source],
            device_id=(x_peer(step) if chunk % 2 == 0 else y_peer(step), pair),
            device_id_type=MESH,
        )

    def second_copy(chunk, step, arrival=False):
        mine = at_y if chunk % 2 == 0 else at_x
        to = lax.rem(mine + step, SIDE)
        source = to if arrival else mine
        return pltpu.make_async_remote_copy(
            src_ref=first_out.at[chunk, pl.ds(pl.multiple_of(to * 16, 16), 16), :],
            dst_ref=second_in.at[chunk, source],
            send_sem=second_send.at[chunk, step],
            recv_sem=second_recv.at[chunk, source],
            device_id=(y_peer(step) if chunk % 2 == 0 else x_peer(step), pair),
            device_id_type=MESH,
        )

    def multiply(chunk):
        @pl.loop(1, PAIRS)
        def _(step):
            pair_arrival(chunk, step).wait_recv()

        @pl.loop(0, columns // width)
        def _(tile):
            where = pl.ds(pl.multiple_of(tile * width, width), width)
            sums[chunk, :, where] = jnp.dot(regrouped[chunk], weights[:, where], preferred_element_type=F32)

        @pl.loop(1, SIDE)
        def _(step):
            first_copy(chunk, step).start()

    def add_first(chunk):
        @pl.loop(1, SIDE)
        def _(step):
            first_copy(chunk, step, arrival=True).wait_recv()

        mine = at_x if chunk % 2 == 0 else at_y
        first_in[chunk, mine] = sums[chunk, pl.ds(pl.multiple_of(mine * SIDE, SIDE), SIDE), :]
        for tile in range(columns // LANES):
            lanes = slice(tile * LANES, (tile + 1) * LANES)
            total = first_in[chunk, 0, :, lanes]
            for source in range(1, SIDE):
                total = total + first_in[chunk, source, :, lanes]
            first_out[chunk, pl.ds(tile, SIDE, stride=16), :] = total

        @pl.loop(1, SIDE)
        def _(step):
            second_copy(chunk, step).start()

    def add_second(chunk):
        @pl.loop(1, SIDE)
        def _(step):
            second_copy(chunk, step, arrival=True).wait_recv()

        mine = at_y if chunk % 2 == 0 else at_x
        second_in[chunk, mine] = first_out[chunk, pl.ds(pl.multiple_of(mine * 16, 16), 16), :]
        total = second_in[chunk, 0]
        for source in range(1, SIDE):
            total = total + second_in[chunk, source]
        panel[chunk * 16 : (chunk + 1) * 16, :] = total

    for turn in range(ROWS + 2):
        if turn < ROWS:
            multiply(turn)
        if 0 <= turn - 1 < ROWS:
            add_first(turn - 1)
        if 0 <= turn - 2 < ROWS:
            add_second(turn - 2)

    row = lax.broadcasted_iota(jnp.int32, (ROWS, columns), 0)
    row_gap = jnp.zeros((ROWS, columns), F32)
    for r in range(ROWS):
        row_gap = jnp.where(row == r, virt_scalar[row_vir[r]] - occ_scalar[row_occ[r]], row_gap)
    cycle = jnp.concatenate([panel[pl.ds(tile, ROWS, stride=16), :] for tile in range(columns // LANES)], axis=1)
    out_ref[...] = cycle / (row_gap + col_gap[...])

    for chunk in range(ROWS):

        @pl.loop(1, PAIRS)
        def _(step):
            pair_copy(chunk, step).wait_send()

        @pl.loop(1, SIDE)
        def _(step):
            first_copy(chunk, step).wait_send()
            second_copy(chunk, step).wait_send()


def local(
    amps,
    intermediate,
    row_irrep,
    kc_irrep,
    row_occ,
    row_vir,
    col_occ,
    col_vir,
    occ_energy,
    virt_energy,
):
    depth, columns = intermediate.shape
    vmem = pl.BlockSpec(memory_space=pltpu.VMEM)
    smem = pl.BlockSpec(memory_space=pltpu.SMEM)
    anywhere = pl.BlockSpec(memory_space=pl.ANY)
    dma = pltpu.SemaphoreType.DMA
    panel_update = pl.pallas_call(
        kernel,
        out_shape=jax.ShapeDtypeStruct((ROWS, columns), F32),
        in_specs=[anywhere, anywhere, smem, vmem, smem, smem, vmem, vmem, smem, smem, vmem, vmem],
        out_specs=vmem,
        scratch_shapes=[
            pltpu.VMEM(amps.shape, BF16),
            pltpu.VMEM((depth, columns), BF16),
            pltpu.VMEM((ROWS, PAIRS, PLANE, LANES), BF16),
            pltpu.VMEM((ROWS, PLANE, depth), BF16),
            pltpu.VMEM((ROWS, PLANE, columns), F32),
            pltpu.VMEM((ROWS, SIDE, SIDE, columns), F32),
            pltpu.VMEM((ROWS, SIDE * 16, LANES), F32),
            pltpu.VMEM((ROWS, SIDE, 16, LANES), F32),
            pltpu.VMEM((ROWS * 16, LANES), F32),
            pltpu.VMEM((1, 1536), F32),
            pltpu.VMEM((1, 256), F32),
            pltpu.VMEM((1, columns), F32),
            dma,
            dma,
            dma((ROWS, PAIRS)),
            dma((ROWS, PAIRS)),
            dma((ROWS, SIDE)),
            dma((ROWS, SIDE)),
            dma((ROWS, SIDE)),
            dma((ROWS, SIDE)),
        ],
        compiler_params=pltpu.CompilerParams(
            collective_id=0, has_side_effects=True, vmem_limit_bytes=40 * 1024 * 1024
        ),
        cost_estimate=pl.CostEstimate(flops=2 * amps.shape[0] * amps.shape[1] * columns, bytes_accessed=9 << 20, transcendentals=0),
    )(
        amps,
        intermediate,
        row_irrep,
        kc_irrep[None, :],
        row_occ,
        row_vir,
        col_occ[None, :],
        col_vir[None, :],
        occ_energy,
        virt_energy,
        occ_energy[None, :],
        virt_energy[None, :],
    )
    return panel_update.astype(BF16)


def solution(mesh):
    return jax.shard_map(
        local,
        mesh=mesh,
        in_specs=(
            P(None, ("bulk", "pair")),
            P("bulk", None),
            P(),
            P(("bulk", "pair")),
            P(("pair", "bulk")),
            P(("pair", "bulk")),
            P(),
            P(),
            P(),
            P(),
        ),
        out_specs=P(("pair", "bulk"), None),
        check_vma=False,
    )
```

```python
import functools

import jax
import jax.numpy as jnp
from jax import lax
from jax.experimental import pallas as pl
from jax.experimental.pallas import tpu as pltpu
from jax.sharding import PartitionSpec as P

MESH = pl.DeviceIdType.MESH
F32 = jnp.float32
BF16 = jnp.bfloat16

SIDE = 8
PAIRS = 16
ROWS = 4
PLANE = SIDE * SIDE
LANES = 128
IRB = 64
CODES = 32767.0


def split_gather(table, labels):
    size = table.shape[1]
    whole = jnp.broadcast_to(table, (16, size))
    high = whole.astype(BF16).astype(F32)
    rest = whole - high
    middle = rest.astype(BF16).astype(F32)
    low = rest - middle
    part = lax.broadcasted_iota(jnp.int32, (16, size), 0)
    parts = jnp.where(part == 0, high, jnp.where(part == 1, middle, jnp.where(part == 2, low, 0.0))).astype(BF16)
    place = lax.broadcasted_iota(jnp.int32, (size, labels.shape[1]), 0)
    chosen = jnp.where(place == labels, 1.0, 0.0).astype(BF16)
    got = jnp.dot(parts, chosen, preferred_element_type=F32)
    return got[0:1, :] + (got[1:2, :] + got[2:3, :])


def kernel(
    amps_hbm,
    weights_hbm,
    row_irrep_hbm,
    kc_irrep_hbm,
    row_occ_hbm,
    row_vir_hbm,
    col_occ_hbm,
    col_vir_hbm,
    occ_hbm,
    virt_hbm,
    out_ref,
    row_irrep,
    kc_irrep,
    row_occ,
    row_vir,
    col_occ,
    col_vir,
    occ_scalar,
    virt_scalar,
    occ_vector,
    virt_vector,
    amps,
    weights,
    outgoing,
    regrouped,
    sums_x,
    sums_y,
    coded_out,
    coded_in,
    scale_out,
    scale_in,
    first_out,
    second_in,
    panel,
    virt_table,
    occ_table,
    col_gap,
    small_sem,
    amps_sem,
    weights_sem,
    pair_send,
    pair_recv,
    coded_send,
    coded_recv,
    scale_send,
    scale_recv,
    second_send,
    second_recv,
):
    bulk = lax.axis_index("bulk")
    pair = lax.axis_index("pair")
    at_y, at_x = lax.div(bulk, SIDE), lax.rem(bulk, SIDE)
    columns = weights.shape[1]

    amps_copy = pltpu.make_async_copy(amps_hbm, amps, amps_sem)
    amps_copy.start()
    small = [
        (row_irrep_hbm, row_irrep),
        (kc_irrep_hbm, kc_irrep),
        (row_occ_hbm, row_occ),
        (row_vir_hbm, row_vir),
        (col_occ_hbm, col_occ),
        (col_vir_hbm, col_vir),
        (occ_hbm, occ_scalar),
        (virt_hbm, virt_scalar),
        (occ_hbm, occ_vector),
        (virt_hbm, virt_vector),
    ]
    small_copies = [pltpu.make_async_copy(a, b, small_sem.at[i]) for i, (a, b) in enumerate(small)]
    for copy in small_copies:
        copy.start()
    weights_copy = pltpu.make_async_copy(weights_hbm, weights, weights_sem)
    weights_copy.start()

    def pair_peer(step):
        return lax.rem(pair + step, PAIRS)

    def x_peer(step):
        return at_y * SIDE + lax.rem(at_x + step, SIDE)

    def y_peer(step):
        return lax.rem(at_y + step, SIDE) * SIDE + at_x

    barrier = pltpu.get_barrier_semaphore()

    @pl.loop(1, PAIRS)
    def _(step):
        pl.semaphore_signal(barrier, inc=1, device_id=(bulk, pair_peer(step)), device_id_type=MESH)

    @pl.loop(1, SIDE)
    def _(step):
        pl.semaphore_signal(barrier, inc=1, device_id=(x_peer(step), pair), device_id_type=MESH)
        pl.semaphore_signal(barrier, inc=1, device_id=(y_peer(step), pair), device_id_type=MESH)

    block = ROWS * PLANE
    new_place = lax.broadcasted_iota(jnp.int32, (block, block), 0)
    old_place = lax.broadcasted_iota(jnp.int32, (block, block), 1)
    chunk_of, x_of, y_of = new_place >> 6, (new_place >> 3) & 7, new_place & 7
    reorder = jnp.where(old_place == y_of * (SIDE * ROWS) + x_of * ROWS + chunk_of, 1.0, 0.0).astype(BF16)
    for copy in small_copies[:2]:
        copy.wait()
    kc = kc_irrep[...]

    amps_copy.wait()

    def prepare(owner):
        kept = []
        for part in range(block // IRB):
            label = row_irrep[owner * block + part * IRB]
            keep = jnp.where(kc == label, 1.0, 0.0)
            begin = pl.multiple_of(owner * block + part * IRB, IRB)
            kept.append((amps[pl.ds(begin, IRB), :].astype(F32) * keep).astype(BF16))
        moved = jnp.dot(reorder, jnp.concatenate(kept, axis=0), preferred_element_type=F32).astype(BF16)
        for chunk in range(ROWS):
            outgoing[chunk, owner] = moved[chunk * PLANE : (chunk + 1) * PLANE, :]

    @pl.loop(0, PAIRS)
    def _(owner):
        prepare(owner)

    pl.semaphore_wait(barrier, PAIRS - 1 + 2 * (SIDE - 1))

    mine_columns = pl.ds(pl.multiple_of(pair * LANES, LANES), LANES)

    for chunk in range(ROWS):

        @pl.loop(1, PAIRS)
        def _(step):
            peer = pair_peer(step)
            pltpu.make_async_remote_copy(
                src_ref=outgoing.at[chunk, peer],
                dst_ref=regrouped.at[chunk, :, mine_columns],
                send_sem=pair_send.at[chunk],
                recv_sem=pair_recv.at[chunk],
                device_id=(bulk, peer),
                device_id_type=MESH,
            ).start()

    def all_of(ref, count, send_sem, recv_sem):
        part = ref.at[pl.ds(0, count)]
        return pltpu.make_async_remote_copy(
            src_ref=part, dst_ref=part, send_sem=send_sem, recv_sem=recv_sem, device_id=(bulk, pair_peer(1)), device_id_type=MESH
        )

    def all_pairs(chunk):
        return all_of(outgoing.at[chunk], PAIRS - 1, pair_send.at[chunk], pair_recv.at[chunk])

    for chunk in range(ROWS):
        regrouped[chunk, :, mine_columns] = outgoing[chunk, pair]

    for copy in small_copies[2:]:
        copy.wait()
    virt_table[...] = jnp.zeros_like(virt_table)
    occ_table[...] = jnp.zeros_like(occ_table)
    virt_table[:, 0 : virt_vector.shape[0]] = virt_vector[...].reshape(1, virt_vector.shape[0])
    occ_table[:, 0 : occ_vector.shape[0]] = occ_vector[...].reshape(1, occ_vector.shape[0])
    width = 256

    @pl.loop(0, columns // width)
    def _(tile):
        where = pl.ds(pl.multiple_of(tile * width, width), width)
        col_gap[:, where] = split_gather(virt_table[...], col_vir[:, where]) - split_gather(occ_table[...], col_occ[:, where])

    weights_copy.wait()

    half_width = columns // 2
    tiles = half_width // LANES

    def along(half, step):
        return x_peer(step) if half == 0 else y_peer(step)

    def place(half):
        return at_x if half == 0 else at_y

    def multiply(chunk, half):
        @pl.loop(0, half_width // width)
        def _(tile):
            where = pl.ds(pl.multiple_of(half * half_width + tile * width, width), width)
            product = jnp.dot(regrouped[chunk], weights[:, where], preferred_element_type=F32)
            if half == 0:
                sums_x[chunk, :, pl.ds(pl.multiple_of(tile * width, width), width)] = product
            else:
                for part in range(width // LANES):
                    sums_y[chunk, tile * (width // LANES) + part] = product[:, part * LANES : (part + 1) * LANES]

    def pieces(chunk, half, to):
        if half == 0:
            rows = pl.ds(pl.multiple_of(to * SIDE, SIDE), SIDE)
            return [sums_x[chunk, rows, tile * LANES : (tile + 1) * LANES] for tile in range(tiles)]
        return [sums_y[chunk, tile, pl.ds(to, SIDE, stride=SIDE), :] for tile in range(tiles)]

    def send_first(chunk, half):
        whole = sums_x[chunk] if half == 0 else sums_y[chunk].reshape(tiles * PLANE, LANES)
        top = jnp.maximum(jnp.max(jnp.abs(whole), axis=(0, 1), keepdims=True), 1e-33)
        scale_out[chunk, half] = jnp.broadcast_to(top * (1.0 / CODES), (1, LANES))
        factor = jnp.broadcast_to(CODES / top, (2 * SIDE, LANES))

        @pl.loop(1, SIDE)
        def _(step):
            to = lax.rem(place(half) + step, SIDE)
            given = pieces(chunk, half, to)
            for tile in range(tiles // 2):
                pair_of = jnp.concatenate([given[tile], given[tile + tiles // 2]], axis=0)
                codes = jnp.round(pair_of * factor).astype(jnp.int32).astype(jnp.int16)
                coded_out[chunk, half, to, :, tile * LANES : (tile + 1) * LANES] = codes
            pltpu.make_async_remote_copy(
                src_ref=scale_out.at[chunk, half],
                dst_ref=scale_in.at[chunk, half, place(half)],
                send_sem=scale_send.at[chunk, half],
                recv_sem=scale_recv.at[chunk, half],
                device_id=(along(half, step), pair),
                device_id_type=MESH,
            ).start()
            pltpu.make_async_remote_copy(
                src_ref=coded_out.at[chunk, half, to],
                dst_ref=coded_in.at[chunk, half, place(half)],
                send_sem=coded_send.at[chunk, half],
                recv_sem=coded_recv.at[chunk, half],
                device_id=(along(half, step), pair),
                device_id_type=MESH,
            ).start()

    def all_scales(chunk, half):
        return all_of(scale_in.at[chunk, half], SIDE - 1, scale_send.at[chunk, half], scale_recv.at[chunk, half])

    def all_coded(chunk, half):
        return all_of(coded_in.at[chunk, half], SIDE - 1, coded_send.at[chunk, half], coded_recv.at[chunk, half])

    def all_second(chunk, half):
        return all_of(second_in.at[chunk, half], SIDE - 1, second_send.at[chunk, half], second_recv.at[chunk, half])

    def add_first(chunk, half):
        all_scales(chunk, half).wait_recv()
        all_coded(chunk, half).wait_recv()
        own = pieces(chunk, half, place(half))
        start = tuple(jnp.concatenate([own[tile], own[tile + tiles // 2]], axis=0) for tile in range(tiles // 2))

        def add(step, totals):
            source = lax.rem(place(half) + step, SIDE)
            scale = scale_in[chunk, half, source]
            return tuple(
                total + coded_in[chunk, half, source, :, tile * LANES : (tile + 1) * LANES].astype(jnp.int32).astype(F32) * scale
                for tile, total in enumerate(totals)
            )

        totals = lax.fori_loop(1, SIDE, add, start)
        for tile, total in enumerate(totals):
            first_out[chunk, half, pl.ds(tile, SIDE, stride=tiles), :] = total[:SIDE, :]
            first_out[chunk, half, pl.ds(tile + tiles // 2, SIDE, stride=tiles), :] = total[SIDE:, :]

        @pl.loop(1, SIDE)
        def _(step):
            mine = place(1 - half)
            to = lax.rem(mine + step, SIDE)
            pltpu.make_async_remote_copy(
                src_ref=first_out.at[chunk, half, pl.ds(pl.multiple_of(to * tiles, tiles), tiles), :],
                dst_ref=second_in.at[chunk, half, mine],
                send_sem=second_send.at[chunk, half],
                recv_sem=second_recv.at[chunk, half],
                device_id=(along(1 - half, step), pair),
                device_id_type=MESH,
            ).start()

    def add_second(chunk, half):
        all_second(chunk, half).wait_recv()
        mine = place(1 - half)
        own = first_out[chunk, half, pl.ds(pl.multiple_of(mine * tiles, tiles), tiles), :]
        total = lax.fori_loop(1, SIDE, lambda step, t: t + second_in[chunk, half, lax.rem(mine + step, SIDE)], own)
        begin = (2 * chunk + half) * tiles
        panel[begin : begin + tiles, :] = total

    for turn in range(ROWS + 2):
        if turn < ROWS:
            all_pairs(turn).wait_recv()
            for half in range(2):
                multiply(turn, half)
                send_first(turn, half)
        if 0 <= turn - 1 < ROWS:
            for half in range(2):
                add_first(turn - 1, half)
        if turn == ROWS:
            for chunk in range(ROWS):
                all_pairs(chunk).wait_send()
            for chunk in range(ROWS):
                for half in range(2):
                    all_scales(chunk, half).wait_send()
                    all_coded(chunk, half).wait_send()
        if 0 <= turn - 2 < ROWS:
            for half in range(2):
                add_second(turn - 2, half)

    row = lax.broadcasted_iota(jnp.int32, (ROWS, columns), 0)
    row_gap = jnp.zeros((ROWS, columns), F32)
    for r in range(ROWS):
        row_gap = jnp.where(row == r, virt_scalar[row_vir[r]] - occ_scalar[row_occ[r]], row_gap)
    cycle = jnp.concatenate([panel[pl.ds(tile, ROWS, stride=16), :] for tile in range(columns // LANES)], axis=1)
    out_ref[...] = cycle / (row_gap + col_gap[...])
    for chunk in range(ROWS):
        for half in range(2):
            all_second(chunk, half).wait_send()


def local(
    amps,
    intermediate,
    row_irrep,
    kc_irrep,
    row_occ,
    row_vir,
    col_occ,
    col_vir,
    occ_energy,
    virt_energy,
):
    depth, columns = intermediate.shape
    vmem = pl.BlockSpec(memory_space=pltpu.VMEM)
    anywhere = pl.BlockSpec(memory_space=pltpu.HBM)
    dma = pltpu.SemaphoreType.DMA
    panel_update = pl.pallas_call(
        kernel,
        out_shape=jax.ShapeDtypeStruct((ROWS, columns), F32),
        in_specs=[anywhere] * 10,
        out_specs=vmem,
        scratch_shapes=[
            pltpu.SMEM(row_irrep.shape, jnp.int32),
            pltpu.VMEM((1, LANES), jnp.int32),
            pltpu.SMEM((ROWS,), jnp.int32),
            pltpu.SMEM((ROWS,), jnp.int32),
            pltpu.VMEM((1, columns), jnp.int32),
            pltpu.VMEM((1, columns), jnp.int32),
            pltpu.SMEM(occ_energy.shape, F32),
            pltpu.SMEM(virt_energy.shape, F32),
            pltpu.VMEM(occ_energy.shape, F32),
            pltpu.VMEM(virt_energy.shape, F32),
            pltpu.VMEM(amps.shape, BF16),
            pltpu.VMEM((depth, columns), BF16),
            pltpu.VMEM((ROWS, PAIRS, PLANE, LANES), BF16),
            pltpu.VMEM((ROWS, PLANE, depth), BF16),
            pltpu.VMEM((ROWS, PLANE, columns // 2), F32),
            pltpu.VMEM((ROWS, columns // 2 // LANES, PLANE, LANES), F32),
            pltpu.VMEM((ROWS, 2, SIDE, 16, columns // 4), jnp.int16),
            pltpu.VMEM((ROWS, 2, SIDE, 16, columns // 4), jnp.int16),
            pltpu.VMEM((ROWS, 2, 1, LANES), F32),
            pltpu.VMEM((ROWS, 2, SIDE, 1, LANES), F32),
            pltpu.VMEM((ROWS, 2, SIDE * columns // 2 // LANES, LANES), F32),
            pltpu.VMEM((ROWS, 2, SIDE, columns // 2 // LANES, LANES), F32),
            pltpu.VMEM((ROWS * columns // LANES, LANES), F32),
            pltpu.VMEM((1, 1536), F32),
            pltpu.VMEM((1, 256), F32),
            pltpu.VMEM((1, columns), F32),
            dma((10,)),
            dma,
            dma,
            dma((ROWS,)),
            dma((ROWS,)),
            dma((ROWS, 2)),
            dma((ROWS, 2)),
            dma((ROWS, 2)),
            dma((ROWS, 2)),
            dma((ROWS, 2)),
            dma((ROWS, 2)),
        ],
        compiler_params=pltpu.CompilerParams(
            collective_id=0, has_side_effects=True, vmem_limit_bytes=63 * 1024 * 1024
        ),
        cost_estimate=pl.CostEstimate(flops=2 * amps.shape[0] * amps.shape[1] * columns, bytes_accessed=9 << 20, transcendentals=0),
    )(
        amps,
        intermediate,
        row_irrep,
        kc_irrep[None, :],
        row_occ,
        row_vir,
        col_occ[None, :],
        col_vir[None, :],
        occ_energy,
        virt_energy,
    )
    return panel_update.astype(BF16)


def solution(mesh):
    return jax.shard_map(
        local,
        mesh=mesh,
        in_specs=(
            P(None, ("bulk", "pair")),
            P("bulk", None),
            P(),
            P(("bulk", "pair")),
            P(("pair", "bulk")),
            P(("pair", "bulk")),
            P(),
            P(),
            P(),
            P(),
        ),
        out_specs=P(("pair", "bulk"), None),
        check_vma=False,
    )
```

```python
import functools

import jax
import jax.numpy as jnp
from jax import lax
from jax.experimental import pallas as pl
from jax.experimental.pallas import tpu as pltpu
from jax.sharding import PartitionSpec as P

MESH = pl.DeviceIdType.MESH
F32 = jnp.float32
BF16 = jnp.bfloat16

SIDE = 8
PAIRS = 16
ROWS = 4
PLANE = SIDE * SIDE
LANES = 128
IRB = 64
CODES = 32767.0


def split_gather(table, labels):
    size = table.shape[1]
    whole = jnp.broadcast_to(table, (16, size))
    high = whole.astype(BF16).astype(F32)
    rest = whole - high
    middle = rest.astype(BF16).astype(F32)
    low = rest - middle
    part = lax.broadcasted_iota(jnp.int32, (16, size), 0)
    parts = jnp.where(part == 0, high, jnp.where(part == 1, middle, jnp.where(part == 2, low, 0.0))).astype(BF16)
    place = lax.broadcasted_iota(jnp.int32, (size, labels.shape[1]), 0)
    chosen = jnp.where(place == labels, 1.0, 0.0).astype(BF16)
    got = jnp.dot(parts, chosen, preferred_element_type=F32)
    return got[0:1, :] + (got[1:2, :] + got[2:3, :])


def kernel(
    amps_hbm,
    weights_hbm,
    row_irrep_hbm,
    kc_irrep_hbm,
    row_occ_hbm,
    row_vir_hbm,
    col_occ_hbm,
    col_vir_hbm,
    occ_hbm,
    virt_hbm,
    out_ref,
    row_irrep,
    kc_irrep,
    row_occ,
    row_vir,
    col_occ,
    col_vir,
    occ_scalar,
    virt_scalar,
    occ_vector,
    virt_vector,
    amps,
    weights,
    outgoing,
    regrouped,
    sums,
    coded_out,
    coded_in,
    scale_out,
    scale_in,
    first_out,
    second_in,
    panel,
    virt_table,
    occ_table,
    col_gap,
    small_sem,
    amps_sem,
    weights_sem,
    pair_send,
    pair_recv,
    coded_send,
    coded_recv,
    scale_send,
    scale_recv,
    second_send,
    second_recv,
    pair_entered,
    plane_entered,
):
    bulk = lax.axis_index("bulk")
    pair = lax.axis_index("pair")
    at_y, at_x = lax.div(bulk, SIDE), lax.rem(bulk, SIDE)
    columns = weights.shape[1]

    amps_copy = pltpu.make_async_copy(amps_hbm, amps, amps_sem)
    amps_copy.start()
    small = [
        (row_irrep_hbm, row_irrep),
        (kc_irrep_hbm, kc_irrep),
        (row_occ_hbm, row_occ),
        (row_vir_hbm, row_vir),
        (col_occ_hbm, col_occ),
        (col_vir_hbm, col_vir),
        (occ_hbm, occ_scalar),
        (virt_hbm, virt_scalar),
        (occ_hbm, occ_vector),
        (virt_hbm, virt_vector),
    ]
    small_copies = [pltpu.make_async_copy(a, b, small_sem.at[i]) for i, (a, b) in enumerate(small)]
    for copy in small_copies:
        copy.start()
    weights_copy = pltpu.make_async_copy(weights_hbm, weights, weights_sem)
    weights_copy.start()

    def x_peer(step):
        return at_y * SIDE + lax.rem(at_x + step, SIDE)

    def y_peer(step):
        return lax.rem(at_y + step, SIDE) * SIDE + at_x

    corner = lax.div(PLANE - bulk, PLANE)
    moving = 14

    def pair_at(rank):
        return jnp.where(rank < moving, lax.rem(rank + corner, moving), rank)

    pair_rank = jnp.where(pair < moving, lax.rem(pair + moving - corner, moving), pair)
    first_pair = lax.div(PAIRS - pair, PAIRS)

    def side_rank(place):
        near = jnp.where(place <= SIDE // 2, 2 * place - 1, 2 * (SIDE - place))
        rank = jnp.where(place == 0, 0, near)
        return lax.rem(rank + (SIDE - 1) * first_pair, SIDE)

    x_rank, y_rank = side_rank(at_x), side_rank(at_y)

    barrier = pltpu.get_barrier_semaphore()

    @pl.loop(pair_rank + 1, PAIRS)
    def _(rank):
        pl.semaphore_signal(barrier, inc=1, device_id=(bulk, pair_at(rank)), device_id_type=MESH)

    @pl.loop(1, SIDE)
    def _(step):
        @pl.when(side_rank(lax.rem(at_x + step, SIDE)) > x_rank)
        def _():
            pl.semaphore_signal(barrier, inc=1, device_id=(x_peer(step), pair), device_id_type=MESH)

        @pl.when(side_rank(lax.rem(at_y + step, SIDE)) > y_rank)
        def _():
            pl.semaphore_signal(barrier, inc=1, device_id=(y_peer(step), pair), device_id_type=MESH)

    block = ROWS * PLANE
    new_place = lax.broadcasted_iota(jnp.int32, (block, block), 0)
    old_place = lax.broadcasted_iota(jnp.int32, (block, block), 1)
    chunk_of, x_of, y_of = new_place >> 6, (new_place >> 3) & 7, new_place & 7
    reorder = jnp.where(old_place == y_of * (SIDE * ROWS) + x_of * ROWS + chunk_of, 1.0, 0.0).astype(BF16)

    def prepare(owner):
        kept = []
        for part in range(block // IRB):
            label = row_irrep[owner * block + part * IRB]
            keep = jnp.where(kc == label, 1.0, 0.0)
            begin = pl.multiple_of(owner * block + part * IRB, IRB)
            kept.append((amps[pl.ds(begin, IRB), :].astype(F32) * keep).astype(BF16))
        moved = jnp.dot(reorder, jnp.concatenate(kept, axis=0), preferred_element_type=F32).astype(BF16)
        outgoing[owner] = moved

    earlier = pair_rank + x_rank + y_rank

    @pl.when(earlier > 0)
    def _():
        pl.semaphore_wait(barrier, earlier)

    @pl.loop(0, pair_rank)
    def _(rank):
        pl.semaphore_signal(pair_entered.at[pair], inc=1, device_id=(bulk, pair_at(rank)), device_id_type=MESH)

    @pl.loop(1, SIDE)
    def _(step):
        @pl.when(side_rank(lax.rem(at_x + step, SIDE)) < x_rank)
        def _():
            pl.semaphore_signal(plane_entered, inc=1, device_id=(x_peer(step), pair), device_id_type=MESH)

        @pl.when(side_rank(lax.rem(at_y + step, SIDE)) < y_rank)
        def _():
            pl.semaphore_signal(plane_entered, inc=1, device_id=(y_peer(step), pair), device_id_type=MESH)

    def lanes_of(source):
        return pl.ds(pl.multiple_of(source * LANES, LANES), LANES)

    def pair_copy(peer, arrival=False):
        return pltpu.make_async_remote_copy(
            src_ref=outgoing.at[peer],
            dst_ref=regrouped.at[:, lanes_of(peer if arrival else pair)],
            send_sem=pair_send,
            recv_sem=pair_recv.at[peer if arrival else pair],
            device_id=(bulk, peer),
            device_id_type=MESH,
        )

    amps_copy.wait()
    for copy in small_copies[:2]:
        copy.wait()
    kc = kc_irrep[...]

    @pl.loop(0, PAIRS // 4)
    def _(four):
        peers = [pair_at(four * 4 + i) for i in range(4)]
        for peer in peers:
            prepare(peer)
        for i, peer in enumerate(peers):

            @pl.when(four * 4 + i < pair_rank)
            def _():
                pair_copy(peer).start()

    regrouped[:, lanes_of(pair)] = outgoing[pair]

    def all_of(ref, count, send_sem, recv_sem):
        part = ref.at[pl.ds(0, count)]
        return pltpu.make_async_remote_copy(
            src_ref=part, dst_ref=part, send_sem=send_sem, recv_sem=recv_sem, device_id=(bulk, lax.rem(pair + 1, PAIRS)), device_id_type=MESH
        )

    for copy in small_copies[2:]:
        copy.wait()
    virt_table[...] = jnp.zeros_like(virt_table)
    occ_table[...] = jnp.zeros_like(occ_table)
    virt_table[:, 0 : virt_vector.shape[0]] = virt_vector[...].reshape(1, virt_vector.shape[0])
    occ_table[:, 0 : occ_vector.shape[0]] = occ_vector[...].reshape(1, occ_vector.shape[0])
    width = 256

    @pl.loop(0, columns // width)
    def _(tile):
        where = pl.ds(pl.multiple_of(tile * width, width), width)
        col_gap[:, where] = split_gather(virt_table[...], col_vir[:, where]) - split_gather(occ_table[...], col_occ[:, where])

    weights_copy.wait()

    def accumulate(turn, add):
        sources = [pair_at(2 * turn), pair_at(2 * turn + 1)]
        for source in sources:

            @pl.when(source != pair)
            def _():
                pair_copy(source, arrival=True).wait_recv()

        rows = jnp.concatenate([regrouped[:, lanes_of(source)] for source in sources], axis=1)

        for tile in range(columns // width):
            where = slice(tile * width, (tile + 1) * width)
            factor = jnp.concatenate([weights[lanes_of(source), where] for source in sources], axis=0)
            product = jnp.dot(rows, factor, preferred_element_type=F32)
            for part in range(width // LANES):
                place = tile * (width // LANES) + part
                new = product[:, part * LANES : (part + 1) * LANES]
                sums[place] = sums[place] + new if add else new

    turns = PAIRS // 2

    def greet(turn):
        for core in range(2):
            rank = 2 * turn + core
            peer = pair_at(rank)

            @pl.when(rank > pair_rank)
            def _():
                pl.semaphore_wait(pair_entered.at[peer], 1)
                pair_copy(peer).start()

    for turn in range(turns):
        greet(turn)
    accumulate(0, False)

    @pl.loop(1, turns)
    def _(turn):
        accumulate(turn, True)

    half_width = columns // 2
    tiles = half_width // LANES

    def along(half, step):
        return x_peer(step) if half == 0 else y_peer(step)

    def place(half):
        return at_x if half == 0 else at_y

    def pieces(chunk, half, to):
        if half == 0:
            rows = pl.ds(pl.multiple_of(chunk * PLANE + to * SIDE, SIDE), SIDE)
        else:
            rows = pl.ds(chunk * PLANE + to, SIDE, stride=SIDE)
        return [sums[half * tiles + tile, rows, :] for tile in range(tiles)]

    def send_first(chunk, half):
        whole = sums[half * tiles : (half + 1) * tiles, chunk * PLANE : (chunk + 1) * PLANE, :].reshape(tiles * PLANE, LANES)
        top = jnp.maximum(jnp.max(jnp.abs(whole), axis=(0, 1), keepdims=True), 1e-33)
        scale_out[chunk, half] = jnp.broadcast_to(top * (1.0 / CODES), (1, LANES))
        factor = jnp.broadcast_to(CODES / top, (2 * SIDE, LANES))

        @pl.loop(1, SIDE)
        def _(step):
            to = lax.rem(place(half) + step, SIDE)
            given = pieces(chunk, half, to)
            for tile in range(tiles // 2):
                pair_of = jnp.concatenate([given[tile], given[tile + tiles // 2]], axis=0)
                codes = jnp.round(pair_of * factor).astype(jnp.int32).astype(jnp.int16)
                coded_out[chunk, half, to, :, tile * LANES : (tile + 1) * LANES] = codes
            pltpu.make_async_remote_copy(
                src_ref=scale_out.at[chunk, half],
                dst_ref=scale_in.at[chunk, half, place(half)],
                send_sem=scale_send.at[chunk, half],
                recv_sem=scale_recv.at[chunk, half],
                device_id=(along(half, step), pair),
                device_id_type=MESH,
            ).start()
            pltpu.make_async_remote_copy(
                src_ref=coded_out.at[chunk, half, to],
                dst_ref=coded_in.at[chunk, half, place(half)],
                send_sem=coded_send.at[chunk, half],
                recv_sem=coded_recv.at[chunk, half],
                device_id=(along(half, step), pair),
                device_id_type=MESH,
            ).start()

    def all_scales(chunk, half):
        return all_of(scale_in.at[chunk, half], SIDE - 1, scale_send.at[chunk, half], scale_recv.at[chunk, half])

    def all_coded(chunk, half):
        return all_of(coded_in.at[chunk, half], SIDE - 1, coded_send.at[chunk, half], coded_recv.at[chunk, half])

    def all_second(chunk, half):
        return all_of(second_in.at[chunk, half], SIDE - 1, second_send.at[chunk, half], second_recv.at[chunk, half])

    def add_first(chunk, half):
        all_scales(chunk, half).wait_recv()
        all_coded(chunk, half).wait_recv()
        own = pieces(chunk, half, place(half))
        start = tuple(jnp.concatenate([own[tile], own[tile + tiles // 2]], axis=0) for tile in range(tiles // 2))

        def add(step, totals):
            source = lax.rem(place(half) + step, SIDE)
            scale = scale_in[chunk, half, source]
            return tuple(
                total + coded_in[chunk, half, source, :, tile * LANES : (tile + 1) * LANES].astype(jnp.int32).astype(F32) * scale
                for tile, total in enumerate(totals)
            )

        totals = lax.fori_loop(1, SIDE, add, start)
        for tile, total in enumerate(totals):
            first_out[chunk, half, pl.ds(tile, SIDE, stride=tiles), :] = total[:SIDE, :]
            first_out[chunk, half, pl.ds(tile + tiles // 2, SIDE, stride=tiles), :] = total[SIDE:, :]

        @pl.loop(1, SIDE)
        def _(step):
            mine = place(1 - half)
            to = lax.rem(mine + step, SIDE)
            pltpu.make_async_remote_copy(
                src_ref=first_out.at[chunk, half, pl.ds(pl.multiple_of(to * tiles, tiles), tiles), :],
                dst_ref=second_in.at[chunk, half, mine],
                send_sem=second_send.at[chunk, half],
                recv_sem=second_recv.at[chunk, half],
                device_id=(along(1 - half, step), pair),
                device_id_type=MESH,
            ).start()

    def add_second(chunk, half):
        all_second(chunk, half).wait_recv()
        mine = place(1 - half)
        own = first_out[chunk, half, pl.ds(pl.multiple_of(mine * tiles, tiles), tiles), :]
        total = lax.fori_loop(1, SIDE, lambda step, t: t + second_in[chunk, half, lax.rem(mine + step, SIDE)], own)
        begin = (2 * chunk + half) * tiles
        panel[begin : begin + tiles, :] = total

    later_in_plane = 2 * (SIDE - 1) - x_rank - y_rank

    @pl.when(later_in_plane > 0)
    def _():
        pl.semaphore_wait(plane_entered, later_in_plane)

    for chunk in range(ROWS):
        for half in range(2):
            send_first(chunk, half)
    for chunk in range(ROWS):
        for half in range(2):
            add_first(chunk, half)
    for chunk in range(ROWS):
        for half in range(2):
            all_scales(chunk, half).wait_send()
            all_coded(chunk, half).wait_send()
    for chunk in range(ROWS):
        for half in range(2):
            add_second(chunk, half)

    row = lax.broadcasted_iota(jnp.int32, (ROWS, columns), 0)
    row_gap = jnp.zeros((ROWS, columns), F32)
    for r in range(ROWS):
        row_gap = jnp.where(row == r, virt_scalar[row_vir[r]] - occ_scalar[row_occ[r]], row_gap)
    cycle = jnp.concatenate([panel[pl.ds(tile, ROWS, stride=16), :] for tile in range(columns // LANES)], axis=1)
    out_ref[...] = cycle / (row_gap + col_gap[...])
    all_of(outgoing, PAIRS - 1, pair_send, pair_recv.at[0]).wait_send()
    for chunk in range(ROWS):
        for half in range(2):
            all_second(chunk, half).wait_send()


def local(
    amps,
    intermediate,
    row_irrep,
    kc_irrep,
    row_occ,
    row_vir,
    col_occ,
    col_vir,
    occ_energy,
    virt_energy,
):
    depth, columns = intermediate.shape
    vmem = pl.BlockSpec(memory_space=pltpu.VMEM)
    anywhere = pl.BlockSpec(memory_space=pltpu.HBM)
    dma = pltpu.SemaphoreType.DMA
    panel_update = pl.pallas_call(
        kernel,
        out_shape=jax.ShapeDtypeStruct((ROWS, columns), F32),
        in_specs=[anywhere] * 10,
        out_specs=vmem,
        scratch_shapes=[
            pltpu.SMEM(row_irrep.shape, jnp.int32),
            pltpu.VMEM((1, LANES), jnp.int32),
            pltpu.SMEM((ROWS,), jnp.int32),
            pltpu.SMEM((ROWS,), jnp.int32),
            pltpu.VMEM((1, columns), jnp.int32),
            pltpu.VMEM((1, columns), jnp.int32),
            pltpu.SMEM(occ_energy.shape, F32),
            pltpu.SMEM(virt_energy.shape, F32),
            pltpu.VMEM(occ_energy.shape, F32),
            pltpu.VMEM(virt_energy.shape, F32),
            pltpu.VMEM(amps.shape, BF16),
            pltpu.VMEM((depth, columns), BF16),
            pltpu.VMEM((PAIRS, ROWS * PLANE, LANES), BF16),
            pltpu.VMEM((ROWS * PLANE, depth), BF16),
            pltpu.VMEM((columns // LANES, ROWS * PLANE, LANES), F32),
            pltpu.VMEM((ROWS, 2, SIDE, 16, columns // 4), jnp.int16),
            pltpu.VMEM((ROWS, 2, SIDE, 16, columns // 4), jnp.int16),
            pltpu.VMEM((ROWS, 2, 1, LANES), F32),
            pltpu.VMEM((ROWS, 2, SIDE, 1, LANES), F32),
            pltpu.VMEM((ROWS, 2, SIDE * columns // 2 // LANES, LANES), F32),
            pltpu.VMEM((ROWS, 2, SIDE, columns // 2 // LANES, LANES), F32),
            pltpu.VMEM((ROWS * columns // LANES, LANES), F32),
            pltpu.VMEM((1, 1536), F32),
            pltpu.VMEM((1, 256), F32),
            pltpu.VMEM((1, columns), F32),
            dma((10,)),
            dma,
            dma,
            dma,
            dma((PAIRS,)),
            dma((ROWS, 2)),
            dma((ROWS, 2)),
            dma((ROWS, 2)),
            dma((ROWS, 2)),
            dma((ROWS, 2)),
            dma((ROWS, 2)),
            pltpu.SemaphoreType.REGULAR((PAIRS,)),
            pltpu.SemaphoreType.REGULAR,
        ],
        compiler_params=pltpu.CompilerParams(
            collective_id=0, has_side_effects=True, vmem_limit_bytes=63 * 1024 * 1024
        ),
        cost_estimate=pl.CostEstimate(flops=2 * amps.shape[0] * amps.shape[1] * columns, bytes_accessed=9 << 20, transcendentals=0),
    )(
        amps,
        intermediate,
        row_irrep,
        kc_irrep[None, :],
        row_occ,
        row_vir,
        col_occ[None, :],
        col_vir[None, :],
        occ_energy,
        virt_energy,
    )
    return panel_update.astype(BF16)


def solution(mesh):
    return jax.shard_map(
        local,
        mesh=mesh,
        in_specs=(
            P(None, ("bulk", "pair")),
            P("bulk", None),
            P(),
            P(("bulk", "pair")),
            P(("pair", "bulk")),
            P(("pair", "bulk")),
            P(),
            P(),
            P(),
            P(),
        ),
        out_specs=P(("pair", "bulk"), None),
        check_vma=False,
    )
```

```python
import functools

import jax
import jax.numpy as jnp
from jax import lax
from jax.experimental import pallas as pl
from jax.experimental.pallas import tpu as pltpu
from jax.sharding import PartitionSpec as P

MESH = pl.DeviceIdType.MESH
F32 = jnp.float32
BF16 = jnp.bfloat16

SIDE = 8
PAIRS = 16
ROWS = 4
PLANE = SIDE * SIDE
LANES = 128
IRB = 64
CODES = 32767.0


def split_gather(table, labels):
    size = table.shape[1]
    whole = jnp.broadcast_to(table, (16, size))
    high = whole.astype(BF16).astype(F32)
    rest = whole - high
    middle = rest.astype(BF16).astype(F32)
    low = rest - middle
    part = lax.broadcasted_iota(jnp.int32, (16, size), 0)
    parts = jnp.where(part == 0, high, jnp.where(part == 1, middle, jnp.where(part == 2, low, 0.0))).astype(BF16)
    place = lax.broadcasted_iota(jnp.int32, (size, labels.shape[1]), 0)
    chosen = jnp.where(place == labels, 1.0, 0.0).astype(BF16)
    got = jnp.dot(parts, chosen, preferred_element_type=F32)
    return got[0:1, :] + (got[1:2, :] + got[2:3, :])


def kernel(
    amps_hbm,
    weights_hbm,
    row_irrep_hbm,
    kc_irrep_hbm,
    row_occ_hbm,
    row_vir_hbm,
    col_occ_hbm,
    col_vir_hbm,
    occ_hbm,
    virt_hbm,
    out_ref,
    row_irrep,
    kc_irrep,
    row_occ,
    row_vir,
    col_occ,
    col_vir,
    occ_scalar,
    virt_scalar,
    occ_vector,
    virt_vector,
    amps,
    weights,
    outgoing,
    regrouped,
    sums,
    coded_out,
    far_in,
    near_in,
    scale_out,
    scale_in,
    relay_scale_out,
    relay_scale_in,
    first_out,
    second_in,
    panel,
    virt_table,
    occ_table,
    col_gap,
    small_sem,
    amps_sem,
    weights_sem,
    pair_send,
    pair_recv,
    coded_send,
    far_recv,
    near_recv,
    scale_send,
    scale_recv,
    relay_scale_send,
    relay_scale_recv,
    second_send,
    second_recv,
    pair_entered,
    plane_entered,
):
    bulk = lax.axis_index("bulk")
    pair = lax.axis_index("pair")
    at_y, at_x = lax.div(bulk, SIDE), lax.rem(bulk, SIDE)
    columns = weights.shape[1]

    amps_copy = pltpu.make_async_copy(amps_hbm, amps, amps_sem)
    amps_copy.start()
    small = [
        (row_irrep_hbm, row_irrep),
        (kc_irrep_hbm, kc_irrep),
        (row_occ_hbm, row_occ),
        (row_vir_hbm, row_vir),
        (col_occ_hbm, col_occ),
        (col_vir_hbm, col_vir),
        (occ_hbm, occ_scalar),
        (virt_hbm, virt_scalar),
        (occ_hbm, occ_vector),
        (virt_hbm, virt_vector),
    ]
    small_copies = [pltpu.make_async_copy(a, b, small_sem.at[i]) for i, (a, b) in enumerate(small)]
    for copy in small_copies:
        copy.start()
    weights_copy = pltpu.make_async_copy(weights_hbm, weights, weights_sem)
    weights_copy.start()

    def x_peer(step):
        return at_y * SIDE + lax.rem(at_x + step, SIDE)

    def y_peer(step):
        return lax.rem(at_y + step, SIDE) * SIDE + at_x

    corner = lax.div(PLANE - bulk, PLANE)
    moving = 14

    def pair_at(rank):
        return jnp.where(rank < moving, lax.rem(rank + corner, moving), rank)

    pair_rank = jnp.where(pair < moving, lax.rem(pair + moving - corner, moving), pair)
    first_pair = lax.div(PAIRS - pair, PAIRS)

    def side_rank(place):
        near = jnp.where(place <= SIDE // 2, 2 * place - 1, 2 * (SIDE - place))
        rank = jnp.where(place == 0, 0, near)
        return lax.rem(rank + (SIDE - 1) * first_pair, SIDE)

    x_rank, y_rank = side_rank(at_x), side_rank(at_y)

    barrier = pltpu.get_barrier_semaphore()

    @pl.loop(pair_rank + 1, PAIRS)
    def _(rank):
        pl.semaphore_signal(barrier, inc=1, device_id=(bulk, pair_at(rank)), device_id_type=MESH)

    @pl.loop(1, SIDE)
    def _(step):
        @pl.when(side_rank(lax.rem(at_x + step, SIDE)) > x_rank)
        def _():
            pl.semaphore_signal(barrier, inc=1, device_id=(x_peer(step), pair), device_id_type=MESH)

        @pl.when(side_rank(lax.rem(at_y + step, SIDE)) > y_rank)
        def _():
            pl.semaphore_signal(barrier, inc=1, device_id=(y_peer(step), pair), device_id_type=MESH)

    block = ROWS * PLANE
    new_place = lax.broadcasted_iota(jnp.int32, (block, block), 0)
    old_place = lax.broadcasted_iota(jnp.int32, (block, block), 1)
    chunk_of, x_of, y_of = new_place >> 6, (new_place >> 3) & 7, new_place & 7
    reorder = jnp.where(old_place == y_of * (SIDE * ROWS) + x_of * ROWS + chunk_of, 1.0, 0.0).astype(BF16)

    def prepare(owner):
        kept = []
        for part in range(block // IRB):
            label = row_irrep[owner * block + part * IRB]
            keep = jnp.where(kc == label, 1.0, 0.0)
            begin = pl.multiple_of(owner * block + part * IRB, IRB)
            kept.append((amps[pl.ds(begin, IRB), :].astype(F32) * keep).astype(BF16))
        moved = jnp.dot(reorder, jnp.concatenate(kept, axis=0), preferred_element_type=F32).astype(BF16)
        outgoing[owner] = moved

    earlier = pair_rank + x_rank + y_rank

    @pl.when(earlier > 0)
    def _():
        pl.semaphore_wait(barrier, earlier)

    @pl.loop(0, pair_rank)
    def _(rank):
        pl.semaphore_signal(pair_entered.at[pair], inc=1, device_id=(bulk, pair_at(rank)), device_id_type=MESH)

    @pl.loop(1, SIDE)
    def _(step):
        @pl.when(side_rank(lax.rem(at_x + step, SIDE)) < x_rank)
        def _():
            pl.semaphore_signal(plane_entered, inc=1, device_id=(x_peer(step), pair), device_id_type=MESH)

        @pl.when(side_rank(lax.rem(at_y + step, SIDE)) < y_rank)
        def _():
            pl.semaphore_signal(plane_entered, inc=1, device_id=(y_peer(step), pair), device_id_type=MESH)

    def lanes_of(source):
        return pl.ds(pl.multiple_of(source * LANES, LANES), LANES)

    def pair_copy(peer, arrival=False):
        return pltpu.make_async_remote_copy(
            src_ref=outgoing.at[peer],
            dst_ref=regrouped.at[:, lanes_of(peer if arrival else pair)],
            send_sem=pair_send,
            recv_sem=pair_recv.at[peer if arrival else pair],
            device_id=(bulk, peer),
            device_id_type=MESH,
        )

    amps_copy.wait()
    for copy in small_copies[:2]:
        copy.wait()
    kc = kc_irrep[...]

    @pl.loop(0, PAIRS // 4)
    def _(four):
        peers = [pair_at(four * 4 + i) for i in range(4)]
        for peer in peers:
            prepare(peer)
        for i, peer in enumerate(peers):

            @pl.when(four * 4 + i < pair_rank)
            def _():
                pair_copy(peer).start()

    regrouped[:, lanes_of(pair)] = outgoing[pair]

    def all_of(ref, count, send_sem, recv_sem):
        part = ref.at[pl.ds(0, count)]
        return pltpu.make_async_remote_copy(
            src_ref=part, dst_ref=part, send_sem=send_sem, recv_sem=recv_sem, device_id=(bulk, lax.rem(pair + 1, PAIRS)), device_id_type=MESH
        )

    for copy in small_copies[2:]:
        copy.wait()
    virt_table[...] = jnp.zeros_like(virt_table)
    occ_table[...] = jnp.zeros_like(occ_table)
    virt_table[:, 0 : virt_vector.shape[0]] = virt_vector[...].reshape(1, virt_vector.shape[0])
    occ_table[:, 0 : occ_vector.shape[0]] = occ_vector[...].reshape(1, occ_vector.shape[0])
    width = 256

    @pl.loop(0, columns // width)
    def _(tile):
        where = pl.ds(pl.multiple_of(tile * width, width), width)
        col_gap[:, where] = split_gather(virt_table[...], col_vir[:, where]) - split_gather(occ_table[...], col_occ[:, where])

    weights_copy.wait()

    def accumulate(turn, add):
        sources = [pair_at(2 * turn), pair_at(2 * turn + 1)]
        for source in sources:

            @pl.when(source != pair)
            def _():
                pair_copy(source, arrival=True).wait_recv()

        rows = jnp.concatenate([regrouped[:, lanes_of(source)] for source in sources], axis=1)

        for tile in range(columns // width):
            where = slice(tile * width, (tile + 1) * width)
            factor = jnp.concatenate([weights[lanes_of(source), where] for source in sources], axis=0)
            product = jnp.dot(rows, factor, preferred_element_type=F32)
            for part in range(width // LANES):
                place = tile * (width // LANES) + part
                new = product[:, part * LANES : (part + 1) * LANES]
                sums[place] = sums[place] + new if add else new

    turns = PAIRS // 2

    def greet(turn):
        for core in range(2):
            rank = 2 * turn + core
            peer = pair_at(rank)

            @pl.when(rank > pair_rank)
            def _():
                pl.semaphore_wait(pair_entered.at[peer], 1)
                pair_copy(peer).start()

    for turn in range(turns):
        greet(turn)
    accumulate(0, False)

    @pl.loop(1, turns)
    def _(turn):
        accumulate(turn, True)

    half_width = columns // 2
    tiles = half_width // LANES

    def along(half, step):
        return x_peer(step) if half == 0 else y_peer(step)

    def place(half):
        return at_x if half == 0 else at_y

    def pieces(chunk, half, to):
        if half == 0:
            rows = pl.ds(pl.multiple_of(chunk * PLANE + to * SIDE, SIDE), SIDE)
        else:
            rows = pl.ds(chunk * PLANE + to, SIDE, stride=SIDE)
        return [sums[half * tiles + tile, rows, :] for tile in range(tiles)]

    ahead = (1, SIDE - 1, 2, SIDE - 2)
    quarter = tiles // 2

    def joined(given):
        return [jnp.concatenate([given[tile], given[tile + quarter]], axis=0) for tile in range(quarter)]

    def block_for(chunk, half, step):
        return joined(pieces(chunk, half, lax.rem(place(half) + step, SIDE)))

    def store_codes(chunk, half, slot, blocks, factor):
        for tile, value in enumerate(blocks):
            codes = jnp.round(value * factor).astype(jnp.int32).astype(jnp.int16)
            coded_out[chunk, half, slot, :, tile * LANES : (tile + 1) * LANES] = codes

    def first_copy(chunk, half, slot, target, recv_sem, step, lanes=slice(None)):
        return pltpu.make_async_remote_copy(
            src_ref=coded_out.at[chunk, half, slot, :, lanes],
            dst_ref=target.at[:, lanes],
            send_sem=coded_send.at[chunk, half],
            recv_sem=recv_sem.at[chunk, half],
            device_id=(along(half, step), pair),
            device_id_type=MESH,
        )

    later_in_plane = 2 * (SIDE - 1) - x_rank - y_rank

    @pl.when(later_in_plane > 0)
    def _():
        pl.semaphore_wait(plane_entered, later_in_plane)

    factors = []
    for half in range(2):
        whole = sums[half * tiles : (half + 1) * tiles].reshape(tiles * block, LANES)
        top = jnp.maximum(jnp.max(jnp.abs(whole), axis=(0, 1), keepdims=True), 1e-33)
        scale_out[half] = jnp.broadcast_to(top * (1.0 / CODES), (1, LANES))
        factors.append(jnp.broadcast_to(CODES / top, (2 * SIDE, LANES)))
        for slot, step in enumerate(ahead):
            pltpu.make_async_remote_copy(
                src_ref=scale_out.at[half],
                dst_ref=scale_in.at[half, slot],
                send_sem=scale_send.at[half],
                recv_sem=scale_recv.at[half],
                device_id=(along(half, step), pair),
                device_id_type=MESH,
            ).start()

    left, right = slice(0, quarter * LANES // 2), slice(quarter * LANES // 2, quarter * LANES)

    @pl.loop(0, ROWS)
    def _(chunk):
        for half in range(2):
            for slot, step in ((0, 3), (1, SIDE - 3), (2, 4)):
                store_codes(chunk, half, slot, block_for(chunk, half, step), factors[half])
            first_copy(chunk, half, 0, far_in.at[chunk, half, 0], far_recv, 1).start()
            first_copy(chunk, half, 1, far_in.at[chunk, half, 1], far_recv, SIDE - 1).start()
            first_copy(chunk, half, 2, far_in.at[chunk, half, 2], far_recv, 2, left).start()
            first_copy(chunk, half, 2, far_in.at[chunk, half, 2], far_recv, SIDE - 2, right).start()

    @pl.loop(0, ROWS)
    def _(chunk):
        for half in range(2):
            for slot, step in ((3, 1), (4, SIDE - 1)):
                store_codes(chunk, half, slot, block_for(chunk, half, step), factors[half])
                first_copy(chunk, half, slot, near_in.at[chunk, half, slot - 3], near_recv, step).start()

    relay_factors = []
    for half in range(2):
        all_of(scale_in.at[half], 4, scale_send.at[half], scale_recv.at[half]).wait_recv()
        for way in range(2):
            bound = scale_out[half] + scale_in[half, way] + scale_in[half, 2 + way]
            relay_scale_out[half, way] = bound
            relay_factors.append(jnp.broadcast_to(1.0 / bound, (2 * SIDE, LANES)))
            pltpu.make_async_remote_copy(
                src_ref=relay_scale_out.at[half, way],
                dst_ref=relay_scale_in.at[half, way],
                send_sem=relay_scale_send.at[half],
                recv_sem=relay_scale_recv.at[half],
                device_id=(along(half, ahead[2 + way]), pair),
                device_id_type=MESH,
            ).start()

    def values(ref, chunk, half, slot, tile):
        return ref[chunk, half, slot, :, tile * LANES : (tile + 1) * LANES].astype(jnp.int32).astype(F32)

    @pl.loop(0, ROWS)
    def _(chunk):
        for half in range(2):
            all_of(far_in.at[chunk, half], 3, coded_send.at[chunk, half], far_recv.at[chunk, half]).wait_recv()
            for way in range(2):
                totals = block_for(chunk, half, ahead[2 + way])
                for tile in range(quarter):
                    totals[tile] = totals[tile] + values(far_in, chunk, half, way, tile) * scale_in[half, way]
                    if tile // (quarter // 2) == way:
                        totals[tile] = totals[tile] + values(far_in, chunk, half, 2, tile) * scale_in[half, 2 + way]
                store_codes(chunk, half, 5 + way, totals, relay_factors[2 * half + way])
                first_copy(chunk, half, 5 + way, near_in.at[chunk, half, 2 + way], near_recv, ahead[2 + way]).start()

    for half in range(2):
        all_of(relay_scale_in.at[half], 2, relay_scale_send.at[half], relay_scale_recv.at[half]).wait_recv()

    def all_second(chunk, half):
        return all_of(second_in.at[chunk, half], SIDE - 1, second_send.at[chunk, half], second_recv.at[chunk, half])

    def add_first(chunk, half):
        all_of(near_in.at[chunk, half], 4, coded_send.at[chunk, half], near_recv.at[chunk, half]).wait_recv()
        totals = block_for(chunk, half, 0)
        for tile in range(quarter):
            for slot in range(4):
                scale = scale_in[half, slot] if slot < 2 else relay_scale_in[half, slot - 2]
                totals[tile] = totals[tile] + values(near_in, chunk, half, slot, tile) * scale
        for tile, total in enumerate(totals):
            first_out[chunk, half, pl.ds(tile, SIDE, stride=tiles), :] = total[:SIDE, :]
            first_out[chunk, half, pl.ds(tile + tiles // 2, SIDE, stride=tiles), :] = total[SIDE:, :]

        @pl.loop(1, SIDE)
        def _(step):
            mine = place(1 - half)
            to = lax.rem(mine + step, SIDE)
            pltpu.make_async_remote_copy(
                src_ref=first_out.at[chunk, half, pl.ds(pl.multiple_of(to * tiles, tiles), tiles), :],
                dst_ref=second_in.at[chunk, half, mine],
                send_sem=second_send.at[chunk, half],
                recv_sem=second_recv.at[chunk, half],
                device_id=(along(1 - half, step), pair),
                device_id_type=MESH,
            ).start()

    def add_second(chunk, half):
        all_second(chunk, half).wait_recv()
        mine = place(1 - half)
        own = first_out[chunk, half, pl.ds(pl.multiple_of(mine * tiles, tiles), tiles), :]
        total = lax.fori_loop(1, SIDE, lambda step, t: t + second_in[chunk, half, lax.rem(mine + step, SIDE)], own)
        panel[pl.ds(pl.multiple_of((2 * chunk + half) * tiles, tiles), tiles), :] = total

    @pl.loop(0, ROWS)
    def _(chunk):
        for half in range(2):
            add_first(chunk, half)

    @pl.loop(0, ROWS)
    def _(chunk):
        for half in range(2):
            add_second(chunk, half)

    row = lax.broadcasted_iota(jnp.int32, (ROWS, columns), 0)
    row_gap = jnp.zeros((ROWS, columns), F32)
    for r in range(ROWS):
        row_gap = jnp.where(row == r, virt_scalar[row_vir[r]] - occ_scalar[row_occ[r]], row_gap)
    cycle = jnp.concatenate([panel[pl.ds(tile, ROWS, stride=16), :] for tile in range(columns // LANES)], axis=1)
    out_ref[...] = cycle / (row_gap + col_gap[...])
    all_of(outgoing, PAIRS - 1, pair_send, pair_recv.at[0]).wait_send()
    for half in range(2):
        all_of(scale_in.at[half], 4, scale_send.at[half], scale_recv.at[half]).wait_send()
        all_of(relay_scale_in.at[half], 2, relay_scale_send.at[half], relay_scale_recv.at[half]).wait_send()

    @pl.loop(0, ROWS)
    def _(chunk):
        for half in range(2):
            all_of(coded_out.at[chunk, half], 7, coded_send.at[chunk, half], far_recv.at[chunk, half]).wait_send()
            all_second(chunk, half).wait_send()


def local(
    amps,
    intermediate,
    row_irrep,
    kc_irrep,
    row_occ,
    row_vir,
    col_occ,
    col_vir,
    occ_energy,
    virt_energy,
):
    depth, columns = intermediate.shape
    vmem = pl.BlockSpec(memory_space=pltpu.VMEM)
    anywhere = pl.BlockSpec(memory_space=pltpu.HBM)
    dma = pltpu.SemaphoreType.DMA
    panel_update = pl.pallas_call(
        kernel,
        out_shape=jax.ShapeDtypeStruct((ROWS, columns), F32),
        in_specs=[anywhere] * 10,
        out_specs=vmem,
        scratch_shapes=[
            pltpu.SMEM(row_irrep.shape, jnp.int32),
            pltpu.VMEM((1, LANES), jnp.int32),
            pltpu.SMEM((ROWS,), jnp.int32),
            pltpu.SMEM((ROWS,), jnp.int32),
            pltpu.VMEM((1, columns), jnp.int32),
            pltpu.VMEM((1, columns), jnp.int32),
            pltpu.SMEM(occ_energy.shape, F32),
            pltpu.SMEM(virt_energy.shape, F32),
            pltpu.VMEM(occ_energy.shape, F32),
            pltpu.VMEM(virt_energy.shape, F32),
            pltpu.VMEM(amps.shape, BF16),
            pltpu.VMEM((depth, columns), BF16),
            pltpu.VMEM((PAIRS, ROWS * PLANE, LANES), BF16),
            pltpu.VMEM((ROWS * PLANE, depth), BF16),
            pltpu.VMEM((columns // LANES, ROWS * PLANE, LANES), F32),
            pltpu.VMEM((ROWS, 2, 7, 16, columns // 4), jnp.int16),
            pltpu.VMEM((ROWS, 2, 3, 16, columns // 4), jnp.int16),
            pltpu.VMEM((ROWS, 2, 4, 16, columns // 4), jnp.int16),
            pltpu.VMEM((2, 1, LANES), F32),
            pltpu.VMEM((2, 4, 1, LANES), F32),
            pltpu.VMEM((2, 2, 1, LANES), F32),
            pltpu.VMEM((2, 2, 1, LANES), F32),
            pltpu.VMEM((ROWS, 2, SIDE * columns // 2 // LANES, LANES), F32),
            pltpu.VMEM((ROWS, 2, SIDE, columns // 2 // LANES, LANES), F32),
            pltpu.VMEM((ROWS * columns // LANES, LANES), F32),
            pltpu.VMEM((1, 1536), F32),
            pltpu.VMEM((1, 256), F32),
            pltpu.VMEM((1, columns), F32),
            dma((10,)),
            dma,
            dma,
            dma,
            dma((PAIRS,)),
            dma((ROWS, 2)),
            dma((ROWS, 2)),
            dma((ROWS, 2)),
            dma((2,)),
            dma((2,)),
            dma((2,)),
            dma((2,)),
            dma((ROWS, 2)),
            dma((ROWS, 2)),
            pltpu.SemaphoreType.REGULAR((PAIRS,)),
            pltpu.SemaphoreType.REGULAR,
        ],
        compiler_params=pltpu.CompilerParams(
            collective_id=0, has_side_effects=True, vmem_limit_bytes=63 * 1024 * 1024
        ),
        cost_estimate=pl.CostEstimate(flops=2 * amps.shape[0] * amps.shape[1] * columns, bytes_accessed=9 << 20, transcendentals=0),
    )(
        amps,
        intermediate,
        row_irrep,
        kc_irrep[None, :],
        row_occ,
        row_vir,
        col_occ[None, :],
        col_vir[None, :],
        occ_energy,
        virt_energy,
    )
    return panel_update.astype(BF16)


def solution(mesh):
    return jax.shard_map(
        local,
        mesh=mesh,
        in_specs=(
            P(None, ("bulk", "pair")),
            P("bulk", None),
            P(),
            P(("bulk", "pair")),
            P(("pair", "bulk")),
            P(("pair", "bulk")),
            P(),
            P(),
            P(),
            P(),
        ),
        out_specs=P(("pair", "bulk"), None),
        check_vma=False,
    )
```

```python
import functools

import jax
import jax.numpy as jnp
from jax import lax
from jax.experimental import pallas as pl
from jax.experimental.pallas import tpu as pltpu
from jax.sharding import PartitionSpec as P

MESH = pl.DeviceIdType.MESH
F32 = jnp.float32
BF16 = jnp.bfloat16

SIDE = 8
PAIRS = 16
ROWS = 4
PLANE = SIDE * SIDE
LANES = 128
IRB = 64
CODES = 32767.0


def split_gather(table, labels):
    size = table.shape[1]
    whole = jnp.broadcast_to(table, (16, size))
    high = whole.astype(BF16).astype(F32)
    rest = whole - high
    middle = rest.astype(BF16).astype(F32)
    low = rest - middle
    part = lax.broadcasted_iota(jnp.int32, (16, size), 0)
    parts = jnp.where(part == 0, high, jnp.where(part == 1, middle, jnp.where(part == 2, low, 0.0))).astype(BF16)
    place = lax.broadcasted_iota(jnp.int32, (size, labels.shape[1]), 0)
    chosen = jnp.where(place == labels, 1.0, 0.0).astype(BF16)
    got = jnp.dot(parts, chosen, preferred_element_type=F32)
    return got[0:1, :] + (got[1:2, :] + got[2:3, :])


def kernel(
    amps_hbm,
    weights_hbm,
    row_irrep_hbm,
    kc_irrep_hbm,
    row_occ_hbm,
    row_vir_hbm,
    col_occ_hbm,
    col_vir_hbm,
    occ_hbm,
    virt_hbm,
    out_ref,
    row_irrep,
    kc_irrep,
    row_occ,
    row_vir,
    col_occ,
    col_vir,
    occ_scalar,
    virt_scalar,
    occ_vector,
    virt_vector,
    amps,
    weights,
    outgoing,
    regrouped,
    sums,
    coded_out,
    far_in,
    near_in,
    scale_out,
    scale_in,
    relay_scale_out,
    relay_scale_in,
    first_out,
    second_in,
    panel,
    virt_table,
    occ_table,
    col_gap,
    small_sem,
    amps_sem,
    weights_sem,
    pair_send,
    pair_recv,
    coded_send,
    far_recv,
    near_recv,
    scale_send,
    scale_recv,
    relay_scale_send,
    relay_scale_recv,
    second_send,
    second_recv,
    pair_entered,
    plane_entered,
):
    bulk = lax.axis_index("bulk")
    pair = lax.axis_index("pair")
    at_y, at_x = lax.div(bulk, SIDE), lax.rem(bulk, SIDE)
    columns = weights.shape[1]

    amps_copy = pltpu.make_async_copy(amps_hbm, amps, amps_sem)
    amps_copy.start()
    small = [
        (row_irrep_hbm, row_irrep),
        (kc_irrep_hbm, kc_irrep),
        (row_occ_hbm, row_occ),
        (row_vir_hbm, row_vir),
        (col_occ_hbm, col_occ),
        (col_vir_hbm, col_vir),
        (occ_hbm, occ_scalar),
        (virt_hbm, virt_scalar),
        (occ_hbm, occ_vector),
        (virt_hbm, virt_vector),
    ]
    small_copies = [pltpu.make_async_copy(a, b, small_sem.at[i]) for i, (a, b) in enumerate(small)]
    for copy in small_copies:
        copy.start()
    weights_copy = pltpu.make_async_copy(weights_hbm, weights, weights_sem)

    def x_peer(step):
        return at_y * SIDE + lax.rem(at_x + step, SIDE)

    def y_peer(step):
        return lax.rem(at_y + step, SIDE) * SIDE + at_x

    corner = lax.div(PLANE - bulk, PLANE)
    moving = 14

    def pair_at(rank):
        return jnp.where(rank < moving, lax.rem(rank + corner, moving), rank)

    pair_rank = jnp.where(pair < moving, lax.rem(pair + moving - corner, moving), pair)
    first_pair = lax.div(PAIRS - pair, PAIRS)

    def side_rank(place):
        near = jnp.where(place <= SIDE // 2, 2 * place - 1, 2 * (SIDE - place))
        rank = jnp.where(place == 0, 0, near)
        return lax.rem(rank + (SIDE - 1) * first_pair, SIDE)

    x_rank, y_rank = side_rank(at_x), side_rank(at_y)

    barrier = pltpu.get_barrier_semaphore()

    @pl.loop(pair_rank + 1, PAIRS)
    def _(rank):
        pl.semaphore_signal(barrier, inc=1, device_id=(bulk, pair_at(rank)), device_id_type=MESH)

    @pl.loop(1, SIDE)
    def _(step):
        @pl.when(side_rank(lax.rem(at_x + step, SIDE)) > x_rank)
        def _():
            pl.semaphore_signal(barrier, inc=1, device_id=(x_peer(step), pair), device_id_type=MESH)

        @pl.when(side_rank(lax.rem(at_y + step, SIDE)) > y_rank)
        def _():
            pl.semaphore_signal(barrier, inc=1, device_id=(y_peer(step), pair), device_id_type=MESH)

    block = ROWS * PLANE
    new_place = lax.broadcasted_iota(jnp.int32, (block, block), 0)
    old_place = lax.broadcasted_iota(jnp.int32, (block, block), 1)
    chunk_of, x_of, y_of = new_place >> 6, (new_place >> 3) & 7, new_place & 7
    reorder = jnp.where(old_place == y_of * (SIDE * ROWS) + x_of * ROWS + chunk_of, 1.0, 0.0).astype(BF16)

    def prepare(owner):
        kept = []
        for part in range(block // IRB):
            label = row_irrep[owner * block + part * IRB]
            keep = jnp.where(kc == label, 1.0, 0.0)
            begin = pl.multiple_of(owner * block + part * IRB, IRB)
            kept.append((amps[pl.ds(begin, IRB), :].astype(F32) * keep).astype(BF16))
        moved = jnp.dot(reorder, jnp.concatenate(kept, axis=0), preferred_element_type=F32).astype(BF16)
        outgoing[owner] = moved

    earlier = pair_rank + x_rank + y_rank

    @pl.when(earlier > 0)
    def _():
        pl.semaphore_wait(barrier, earlier)

    @pl.loop(0, pair_rank)
    def _(rank):
        pl.semaphore_signal(pair_entered.at[pair], inc=1, device_id=(bulk, pair_at(rank)), device_id_type=MESH)

    @pl.loop(1, SIDE)
    def _(step):
        @pl.when(side_rank(lax.rem(at_x + step, SIDE)) < x_rank)
        def _():
            pl.semaphore_signal(plane_entered, inc=1, device_id=(x_peer(step), pair), device_id_type=MESH)

        @pl.when(side_rank(lax.rem(at_y + step, SIDE)) < y_rank)
        def _():
            pl.semaphore_signal(plane_entered, inc=1, device_id=(y_peer(step), pair), device_id_type=MESH)

    def lanes_of(source):
        return pl.ds(pl.multiple_of(source * LANES, LANES), LANES)

    def pair_copy(peer, arrival=False):
        return pltpu.make_async_remote_copy(
            src_ref=outgoing.at[peer],
            dst_ref=regrouped.at[:, lanes_of(peer if arrival else pair)],
            send_sem=pair_send,
            recv_sem=pair_recv.at[peer if arrival else pair],
            device_id=(bulk, peer),
            device_id_type=MESH,
        )

    amps_copy.wait()
    weights_copy.start()
    for copy in small_copies[:2]:
        copy.wait()
    kc = kc_irrep[...]

    @pl.loop(0, PAIRS // 4)
    def _(four):
        peers = [pair_at(four * 4 + i) for i in range(4)]
        for peer in peers:
            prepare(peer)
        for i, peer in enumerate(peers):

            @pl.when(four * 4 + i < pair_rank)
            def _():
                pair_copy(peer).start()

    regrouped[:, lanes_of(pair)] = outgoing[pair]

    def all_of(ref, count, send_sem, recv_sem):
        part = ref.at[pl.ds(0, count)]
        return pltpu.make_async_remote_copy(
            src_ref=part, dst_ref=part, send_sem=send_sem, recv_sem=recv_sem, device_id=(bulk, lax.rem(pair + 1, PAIRS)), device_id_type=MESH
        )

    for copy in small_copies[2:]:
        copy.wait()
    virt_table[...] = jnp.zeros_like(virt_table)
    occ_table[...] = jnp.zeros_like(occ_table)
    virt_table[:, 0 : virt_vector.shape[0]] = virt_vector[...].reshape(1, virt_vector.shape[0])
    occ_table[:, 0 : occ_vector.shape[0]] = occ_vector[...].reshape(1, occ_vector.shape[0])
    width = 256

    @pl.loop(0, columns // width)
    def _(tile):
        where = pl.ds(pl.multiple_of(tile * width, width), width)
        col_gap[:, where] = split_gather(virt_table[...], col_vir[:, where]) - split_gather(occ_table[...], col_occ[:, where])

    weights_copy.wait()

    def accumulate(turn, add):
        sources = [pair_at(2 * turn), pair_at(2 * turn + 1)]
        for source in sources:

            @pl.when(source != pair)
            def _():
                pair_copy(source, arrival=True).wait_recv()

        rows = jnp.concatenate([regrouped[:, lanes_of(source)] for source in sources], axis=1)

        for tile in range(columns // width):
            where = slice(tile * width, (tile + 1) * width)
            factor = jnp.concatenate([weights[lanes_of(source), where] for source in sources], axis=0)
            product = jnp.dot(rows, factor, preferred_element_type=F32)
            for part in range(width // LANES):
                place = tile * (width // LANES) + part
                new = product[:, part * LANES : (part + 1) * LANES]
                sums[place] = sums[place] + new if add else new

    turns = PAIRS // 2

    def greet(turn):
        for core in range(2):
            rank = 2 * turn + core
            peer = pair_at(rank)

            @pl.when(rank > pair_rank)
            def _():
                pl.semaphore_wait(pair_entered.at[peer], 1)
                pair_copy(peer).start()

    for turn in range(turns):
        greet(turn)
    accumulate(0, False)

    @pl.loop(1, turns)
    def _(turn):
        accumulate(turn, True)

    half_width = columns // 2
    tiles = half_width // LANES

    def along(half, step):
        return x_peer(step) if half == 0 else y_peer(step)

    def place(half):
        return at_x if half == 0 else at_y

    def pieces(chunk, half, to):
        if half == 0:
            rows = pl.ds(pl.multiple_of(chunk * PLANE + to * SIDE, SIDE), SIDE)
        else:
            rows = pl.ds(chunk * PLANE + to, SIDE, stride=SIDE)
        return [sums[half * tiles + tile, rows, :] for tile in range(tiles)]

    ahead = (1, SIDE - 1, 2, SIDE - 2)
    quarter = tiles // 2

    def joined(given):
        return [jnp.concatenate([given[tile], given[tile + quarter]], axis=0) for tile in range(quarter)]

    def block_for(chunk, half, step):
        return joined(pieces(chunk, half, lax.rem(place(half) + step, SIDE)))

    def store_codes(chunk, half, slot, blocks, factor):
        for tile, value in enumerate(blocks):
            codes = jnp.round(value * factor).astype(jnp.int32).astype(jnp.int16)
            coded_out[chunk, half, slot, :, tile * LANES : (tile + 1) * LANES] = codes

    def first_copy(chunk, half, slot, target, recv_sem, step, lanes=slice(None)):
        return pltpu.make_async_remote_copy(
            src_ref=coded_out.at[chunk, half, slot, :, lanes],
            dst_ref=target.at[:, lanes],
            send_sem=coded_send.at[chunk, half],
            recv_sem=recv_sem.at[chunk, half],
            device_id=(along(half, step), pair),
            device_id_type=MESH,
        )

    later_in_plane = 2 * (SIDE - 1) - x_rank - y_rank

    @pl.when(later_in_plane > 0)
    def _():
        pl.semaphore_wait(plane_entered, later_in_plane)

    factors = []
    for half in range(2):
        whole = sums[half * tiles : (half + 1) * tiles].reshape(tiles * block, LANES)
        top = jnp.maximum(jnp.max(jnp.abs(whole), axis=(0, 1), keepdims=True), 1e-33)
        scale_out[half] = jnp.broadcast_to(top * (1.0 / CODES), (1, LANES))
        factors.append(jnp.broadcast_to(CODES / top, (2 * SIDE, LANES)))
        for slot, step in enumerate(ahead):
            pltpu.make_async_remote_copy(
                src_ref=scale_out.at[half],
                dst_ref=scale_in.at[half, slot],
                send_sem=scale_send.at[half],
                recv_sem=scale_recv.at[half],
                device_id=(along(half, step), pair),
                device_id_type=MESH,
            ).start()

    left, right = slice(0, quarter * LANES // 2), slice(quarter * LANES // 2, quarter * LANES)

    @pl.loop(0, ROWS)
    def _(chunk):
        for half in range(2):
            for slot, step in ((0, 3), (1, SIDE - 3), (2, 4)):
                store_codes(chunk, half, slot, block_for(chunk, half, step), factors[half])
            first_copy(chunk, half, 0, far_in.at[chunk, half, 0], far_recv, 1).start()
            first_copy(chunk, half, 1, far_in.at[chunk, half, 1], far_recv, SIDE - 1).start()
            first_copy(chunk, half, 2, far_in.at[chunk, half, 2], far_recv, 2, left).start()
            first_copy(chunk, half, 2, far_in.at[chunk, half, 2], far_recv, SIDE - 2, right).start()

    @pl.loop(0, ROWS)
    def _(chunk):
        for half in range(2):
            for slot, step in ((3, 1), (4, SIDE - 1)):
                store_codes(chunk, half, slot, block_for(chunk, half, step), factors[half])
                first_copy(chunk, half, slot, near_in.at[chunk, half, slot - 3], near_recv, step).start()

    relay_factors = []
    for half in range(2):
        all_of(scale_in.at[half], 4, scale_send.at[half], scale_recv.at[half]).wait_recv()
        for way in range(2):
            bound = scale_out[half] + scale_in[half, way] + scale_in[half, 2 + way]
            relay_scale_out[half, way] = bound
            relay_factors.append(jnp.broadcast_to(1.0 / bound, (2 * SIDE, LANES)))
            pltpu.make_async_remote_copy(
                src_ref=relay_scale_out.at[half, way],
                dst_ref=relay_scale_in.at[half, way],
                send_sem=relay_scale_send.at[half],
                recv_sem=relay_scale_recv.at[half],
                device_id=(along(half, ahead[2 + way]), pair),
                device_id_type=MESH,
            ).start()

    def values(ref, chunk, half, slot, tile):
        return ref[chunk, half, slot, :, tile * LANES : (tile + 1) * LANES].astype(jnp.int32).astype(F32)

    @pl.loop(0, ROWS)
    def _(chunk):
        for half in range(2):
            all_of(far_in.at[chunk, half], 3, coded_send.at[chunk, half], far_recv.at[chunk, half]).wait_recv()
            for way in range(2):
                totals = block_for(chunk, half, ahead[2 + way])
                for tile in range(quarter):
                    totals[tile] = totals[tile] + values(far_in, chunk, half, way, tile) * scale_in[half, way]
                    if tile // (quarter // 2) == way:
                        totals[tile] = totals[tile] + values(far_in, chunk, half, 2, tile) * scale_in[half, 2 + way]
                store_codes(chunk, half, 5 + way, totals, relay_factors[2 * half + way])
                first_copy(chunk, half, 5 + way, near_in.at[chunk, half, 2 + way], near_recv, ahead[2 + way]).start()

    for half in range(2):
        all_of(relay_scale_in.at[half], 2, relay_scale_send.at[half], relay_scale_recv.at[half]).wait_recv()

    def all_second(chunk, half):
        return all_of(second_in.at[chunk, half], SIDE - 1, second_send.at[chunk, half], second_recv.at[chunk, half])

    def add_first(chunk, half):
        all_of(near_in.at[chunk, half], 4, coded_send.at[chunk, half], near_recv.at[chunk, half]).wait_recv()
        totals = block_for(chunk, half, 0)
        for tile in range(quarter):
            for slot in range(4):
                scale = scale_in[half, slot] if slot < 2 else relay_scale_in[half, slot - 2]
                totals[tile] = totals[tile] + values(near_in, chunk, half, slot, tile) * scale
        for tile, total in enumerate(totals):
            first_out[chunk, half, pl.ds(tile, SIDE, stride=tiles), :] = total[:SIDE, :]
            first_out[chunk, half, pl.ds(tile + tiles // 2, SIDE, stride=tiles), :] = total[SIDE:, :]

        @pl.loop(1, SIDE)
        def _(step):
            mine = place(1 - half)
            to = lax.rem(mine + step, SIDE)
            pltpu.make_async_remote_copy(
                src_ref=first_out.at[chunk, half, pl.ds(pl.multiple_of(to * tiles, tiles), tiles), :],
                dst_ref=second_in.at[chunk, half, mine],
                send_sem=second_send.at[chunk, half],
                recv_sem=second_recv.at[chunk, half],
                device_id=(along(1 - half, step), pair),
                device_id_type=MESH,
            ).start()

    def add_second(chunk, half):
        all_second(chunk, half).wait_recv()
        mine = place(1 - half)
        own = first_out[chunk, half, pl.ds(pl.multiple_of(mine * tiles, tiles), tiles), :]
        total = lax.fori_loop(1, SIDE, lambda step, t: t + second_in[chunk, half, lax.rem(mine + step, SIDE)], own)
        panel[pl.ds(pl.multiple_of((2 * chunk + half) * tiles, tiles), tiles), :] = total

    @pl.loop(0, ROWS)
    def _(chunk):
        for half in range(2):
            add_first(chunk, half)

    all_of(outgoing, PAIRS - 1, pair_send, pair_recv.at[0]).wait_send()
    for half in range(2):
        all_of(scale_in.at[half], 4, scale_send.at[half], scale_recv.at[half]).wait_send()
        all_of(relay_scale_in.at[half], 2, relay_scale_send.at[half], relay_scale_recv.at[half]).wait_send()

    @pl.loop(0, ROWS)
    def _(chunk):
        for half in range(2):
            all_of(coded_out.at[chunk, half], 7, coded_send.at[chunk, half], far_recv.at[chunk, half]).wait_send()

    @pl.loop(0, ROWS)
    def _(chunk):
        for half in range(2):
            add_second(chunk, half)

    row = lax.broadcasted_iota(jnp.int32, (ROWS, columns), 0)
    row_gap = jnp.zeros((ROWS, columns), F32)
    for r in range(ROWS):
        row_gap = jnp.where(row == r, virt_scalar[row_vir[r]] - occ_scalar[row_occ[r]], row_gap)
    cycle = jnp.concatenate([panel[pl.ds(tile, ROWS, stride=16), :] for tile in range(columns // LANES)], axis=1)
    out_ref[...] = cycle / (row_gap + col_gap[...])

    @pl.loop(0, ROWS)
    def _(chunk):
        for half in range(2):
            all_second(chunk, half).wait_send()


def local(
    amps,
    intermediate,
    row_irrep,
    kc_irrep,
    row_occ,
    row_vir,
    col_occ,
    col_vir,
    occ_energy,
    virt_energy,
):
    depth, columns = intermediate.shape
    vmem = pl.BlockSpec(memory_space=pltpu.VMEM)
    anywhere = pl.BlockSpec(memory_space=pltpu.HBM)
    dma = pltpu.SemaphoreType.DMA
    panel_update = pl.pallas_call(
        kernel,
        out_shape=jax.ShapeDtypeStruct((ROWS, columns), F32),
        in_specs=[anywhere] * 10,
        out_specs=vmem,
        scratch_shapes=[
            pltpu.SMEM(row_irrep.shape, jnp.int32),
            pltpu.VMEM((1, LANES), jnp.int32),
            pltpu.SMEM((ROWS,), jnp.int32),
            pltpu.SMEM((ROWS,), jnp.int32),
            pltpu.VMEM((1, columns), jnp.int32),
            pltpu.VMEM((1, columns), jnp.int32),
            pltpu.SMEM(occ_energy.shape, F32),
            pltpu.SMEM(virt_energy.shape, F32),
            pltpu.VMEM(occ_energy.shape, F32),
            pltpu.VMEM(virt_energy.shape, F32),
            pltpu.VMEM(amps.shape, BF16),
            pltpu.VMEM((depth, columns), BF16),
            pltpu.VMEM((PAIRS, ROWS * PLANE, LANES), BF16),
            pltpu.VMEM((ROWS * PLANE, depth), BF16),
            pltpu.VMEM((columns // LANES, ROWS * PLANE, LANES), F32),
            pltpu.VMEM((ROWS, 2, 7, 16, columns // 4), jnp.int16),
            pltpu.VMEM((ROWS, 2, 3, 16, columns // 4), jnp.int16),
            pltpu.VMEM((ROWS, 2, 4, 16, columns // 4), jnp.int16),
            pltpu.VMEM((2, 1, LANES), F32),
            pltpu.VMEM((2, 4, 1, LANES), F32),
            pltpu.VMEM((2, 2, 1, LANES), F32),
            pltpu.VMEM((2, 2, 1, LANES), F32),
            pltpu.VMEM((ROWS, 2, SIDE * columns // 2 // LANES, LANES), F32),
            pltpu.VMEM((ROWS, 2, SIDE, columns // 2 // LANES, LANES), F32),
            pltpu.VMEM((ROWS * columns // LANES, LANES), F32),
            pltpu.VMEM((1, 1536), F32),
            pltpu.VMEM((1, 256), F32),
            pltpu.VMEM((1, columns), F32),
            dma((10,)),
            dma,
            dma,
            dma,
            dma((PAIRS,)),
            dma((ROWS, 2)),
            dma((ROWS, 2)),
            dma((ROWS, 2)),
            dma((2,)),
            dma((2,)),
            dma((2,)),
            dma((2,)),
            dma((ROWS, 2)),
            dma((ROWS, 2)),
            pltpu.SemaphoreType.REGULAR((PAIRS,)),
            pltpu.SemaphoreType.REGULAR,
        ],
        compiler_params=pltpu.CompilerParams(
            collective_id=0, has_side_effects=True, vmem_limit_bytes=63 * 1024 * 1024
        ),
        cost_estimate=pl.CostEstimate(flops=2 * amps.shape[0] * amps.shape[1] * columns, bytes_accessed=9 << 20, transcendentals=0),
    )(
        amps,
        intermediate,
        row_irrep,
        kc_irrep[None, :],
        row_occ,
        row_vir,
        col_occ[None, :],
        col_vir[None, :],
        occ_energy,
        virt_energy,
    )
    return panel_update.astype(BF16)


def solution(mesh):
    return jax.shard_map(
        local,
        mesh=mesh,
        in_specs=(
            P(None, ("bulk", "pair")),
            P("bulk", None),
            P(),
            P(("bulk", "pair")),
            P(("pair", "bulk")),
            P(("pair", "bulk")),
            P(),
            P(),
            P(),
            P(),
        ),
        out_specs=P(("pair", "bulk"), None),
        check_vma=False,
    )
```
